32 devices in a mesh: feat: 2 (over core), seq: 4 (over z), rows: 4 (over y, x).
Axes of the slice: x: 2, y: 2, z: 4, core: 2. Of those that a mesh axis runs over, the one named last changes fastest.
Arguments:
- tokens: float32 [8, 2048, 2048], P(('feat', 'rows'), 'seq'), may hold values from -6 to 6
- lengths: int32 [8, 8], replicated, may hold values from 1 to 2041, as said below
- gain_one: float32 [2048], replicated, may hold values from 0.5 to 1.5
- w_query: bfloat16 [2048, 256], replicated, may hold values from -0.125 to 0.125
- w_key: bfloat16 [2048, 256], replicated, may hold values from -0.125 to 0.125
- w_value: bfloat16 [2048, 2048], replicated, may hold values from -0.125 to 0.125
- w_out: bfloat16 [2048, 2048], replicated, may hold values from -1 to 1
- gain_two: float32 [2048], replicated, may hold values from 0.5 to 1.5
- w_gate: bfloat16 [2048, 5632], replicated, may hold values from -0.125 to 0.125
- w_up: bfloat16 [2048, 5632], replicated, may hold values from -0.125 to 0.125
- w_down: bfloat16 [5632, 2048], replicated, may hold values from -0.078125 to 0.078125
- cotangent: float32 [8, 2048, 2048], P(('feat', 'rows'), 'seq'), may hold values from -6 to 6
Outputs:
- layer_out: float32 [8, 2048, 2048], P(('feat', 'rows'), 'seq')
- grad_tokens: float32 [8, 2048, 2048], P(('feat', 'rows'), 'seq')
- grad_gain_one: float32 [2048], P(('feat', 'seq', 'rows'))
- grad_query_w: float32 [2048, 256], P(('feat', 'seq', 'rows'))
- grad_key_w: float32 [2048, 256], P(('feat', 'seq', 'rows'))
- grad_value_w: float32 [2048, 2048], P(('feat', 'seq', 'rows'))
- grad_out_w: float32 [2048, 2048], P(('feat', 'seq', 'rows'))
- grad_gain_two: float32 [2048], P(('feat', 'seq', 'rows'))
- grad_gate_w: float32 [2048, 5632], P(('feat', 'seq', 'rows'))
- grad_up_w: float32 [2048, 5632], P(('feat', 'seq', 'rows'))
- grad_down_w: float32 [5632, 2048], P(('feat', 'seq', 'rows'))
The draws below stay inside these ranges and needn't reach their ends.
Inputs may be any that keep to these rules, and one draw needn't show every extreme that they name: Each row of lengths gives, in order, the lengths of 8 documents that together fill one packed row of 2048 tokens. Some rows may hold a document that begins before token 128 and ends after token 1920.
All inputs are finite; a program needn't handle non-finite values.
Results may differ from the reference program's by a relative error of at most 0.0096.
Values may be sent and summed in bfloat16 or wider, within the bound.
No kernel may reach another device: no remote copies, remote signals or barrier semaphores. Data moves between devices by JAX's collectives and lax.ppermute only.
A program may use at most 512 MiB of HBM per device.

```python
import jax
import jax.numpy as jnp
from jax import lax

D = 2048
HEADS = 16
FDIM = 16
VHEAD = 128
FF = 5632
LEN_ROW = 2048
NDOC = 8
ROWS_DEV = 1
QK = 256
ROWS_ALL = 8


def draw_lengths(key, part):
    key = jax.random.fold_in(key, 7)
    order_key, pick_key, lead_key = jax.random.split(key, 3)
    noise = jax.random.randint(order_key, (ROWS_ALL, LEN_ROW - 1), 0, 1 << 18)
    scores = noise * LEN_ROW + jnp.arange(LEN_ROW - 1, dtype=jnp.int32)[None, :]
    order = jnp.argsort(scores, axis=1).astype(jnp.int32)
    cuts = jnp.sort(order[:, :NDOC - 1] + 1, axis=1)
    chosen = jax.random.randint(pick_key, (ROWS_ALL // ROWS_DEV,), 0, ROWS_DEV)
    picked = jnp.arange(ROWS_ALL, dtype=jnp.int32) % ROWS_DEV == jnp.repeat(chosen, ROWS_DEV)
    leading = jax.random.randint(lead_key, (ROWS_ALL, 1), 0, NDOC)
    places = jnp.arange(1, NDOC, dtype=jnp.int32)[None, :]
    spanning = jnp.where(places <= leading, places, LEN_ROW - NDOC + places).astype(jnp.int32)
    cuts = jnp.where(picked[:, None], spanning, cuts)
    edges = jnp.concatenate([jnp.zeros((ROWS_ALL, 1), jnp.int32), cuts, jnp.full((ROWS_ALL, 1), LEN_ROW, jnp.int32)], axis=1)
    return (edges[:, 1:] - edges[:, :-1]).astype(jnp.int32)


def level_of(stream_key, dims, shards, smallest, largest):
    loudness, own = 1.0, jax.random.fold_in(stream_key, 6)
    for position, parts in shards:
        draws = jnp.exp(jax.random.uniform(jax.random.fold_in(own, position), (parts,), jnp.float32, smallest / len(shards), largest / len(shards)))
        loudness = loudness * jnp.repeat(draws, dims[position] // parts).reshape([-1 if axis == position else 1 for axis in range(len(dims))])
    return loudness


def bell_draw(stream_key, extent, scale, reach, shards=(), held_as=jnp.bfloat16):
    entries = jax.random.normal(stream_key, extent, jnp.float32) * scale
    if len(shards) > 0:
        entries = level_of(stream_key, extent, shards, -0.22, 0.18) * entries
    return jnp.clip(entries, min=-reach, max=reach).astype(held_as)


def setup_inputs(seed: int = 0) -> dict:
    streams_of = jax.random.split(jax.random.key(seed), 13)
    tokens = bell_draw(streams_of[0], (ROWS_ALL, LEN_ROW, D), 1.0, 6.0, ((0, 8), (1, 4)), jnp.float32)
    lengths = draw_lengths(jax.random.fold_in(streams_of[12], 71), 0)
    gain_one = jnp.clip(1.0 + 0.1 * jax.random.normal(streams_of[2], (D,), jnp.float32), 0.5, 1.5)
    w_query = bell_draw(streams_of[3], (D, QK), D ** -0.5, 0.125)
    w_key = bell_draw(streams_of[4], (D, QK), D ** -0.5, 0.125)
    w_value = bell_draw(streams_of[5], (D, D), D ** -0.5, 0.125)
    w_out = bell_draw(streams_of[6], (D, D), (D // 64) ** -0.5, 1.0)
    gain_two = jnp.clip(1.0 + 0.1 * jax.random.normal(streams_of[7], (D,), jnp.float32), 0.5, 1.5)
    w_gate = bell_draw(streams_of[8], (D, FF), D ** -0.5, 0.125)
    w_up = bell_draw(streams_of[9], (D, FF), D ** -0.5, 0.125)
    w_down = bell_draw(streams_of[10], (FF, D), FF ** -0.5, 0.078125)
    cotangent = bell_draw(streams_of[11], (ROWS_ALL, LEN_ROW, D), 1.0, 6.0, ((0, 8), (1, 4)), jnp.float32)
    return dict(tokens=tokens, lengths=lengths, gain_one=gain_one, w_query=w_query, w_key=w_key, w_value=w_value, w_out=w_out, gain_two=gain_two, w_gate=w_gate, w_up=w_up, w_down=w_down, cotangent=cotangent)


@jax.custom_vjp
def low(v):
    return lax.optimization_barrier(v.astype(jnp.bfloat16)).astype(jnp.float32)

@jax.custom_vjp
def low_back(v):
    return v

def low_keep(v):
    return (low(v), None)

def low_pass(kept, grad):
    return (grad,)

def back_keep(v):
    return (v, None)

def back_low(kept, grad):
    return (low(grad),)
low.defvjp(low_keep, low_pass)
low_back.defvjp(back_keep, back_low)
eps_norm = 1e-06
highest = lax.Precision.HIGHEST

def normalize(values, gain):
    return values * lax.rsqrt(lax.optimization_barrier(jnp.mean(values * values, axis=-1, keepdims=True)) + eps_norm) * gain

def matmul_high(former, latter):
    return jnp.dot(former, latter, precision=highest)

def taylor(values):
    linear = values * FDIM ** (-0.25)
    square = values[..., :, None] * values[..., None, :] * (2.0 * FDIM) ** (-0.5)
    square = square.reshape(values.shape[:-1] + (FDIM * FDIM,))
    constant_col = jnp.ones(values.shape[:-1] + (1,), jnp.float32)
    return jnp.concatenate([constant_col, linear, square], axis=-1)

def row_layer(row_tokens, row_lengths, gain_one, w_query, w_key, w_value, w_out, gain_two, w_gate, w_up, w_down):
    low_one = low(normalize(row_tokens, gain_one))
    queries = low_back(low(matmul_high(low_one, w_query))).reshape(LEN_ROW, HEADS, FDIM)
    keys_row = low_back(low(matmul_high(low_one, w_key))).reshape(LEN_ROW, HEADS, FDIM)
    values_row = low_back(low(matmul_high(low_one, w_value))).reshape(LEN_ROW, HEADS, VHEAD)
    query_feats = low(taylor(queries))
    key_feats = low(taylor(keys_row))
    starts = (jnp.cumsum(row_lengths) - row_lengths).astype(jnp.int32)
    places = jnp.arange(LEN_ROW, dtype=jnp.int32)
    doc_ids = lax.optimization_barrier(jnp.sum((starts[None, :] <= places[:, None]).astype(jnp.int32), axis=1))
    allowed = ((doc_ids[:, None] == doc_ids[None, :]) & (places[None, :] <= places[:, None])).astype(jnp.float32)
    scores = jnp.einsum('thf,shf->hts', query_feats, key_feats, precision=highest) * allowed[None]
    numerator = jnp.einsum('hts,she->the', scores, values_row, precision=highest)
    denominator = jnp.transpose(lax.optimization_barrier(jnp.sum(scores, axis=-1)))
    mixed_heads = (numerator / denominator[:, :, None]).reshape(LEN_ROW, D)
    middle = row_tokens + low_back(matmul_high(low(mixed_heads), w_out))
    low_two = low(normalize(middle, gain_two))
    gate_act = low_back(matmul_high(low_two, w_gate))
    up_act = low_back(matmul_high(low_two, w_up))
    hidden = low(jax.nn.silu(gate_act) * up_act)
    return middle + low_back(matmul_high(hidden, w_down))

def reference(tokens, lengths, gain_one, w_query, w_key, w_value, w_out, gain_two, w_gate, w_up, w_down, cotangent):
    layer_step = jax.checkpoint(row_layer)

    def forward(all_tokens, gain_first, query_w, key_w, value_w, out_w, gain_second, gate_w, up_w, down_w):

        def one_row(carried, row_item):
            return (carried, layer_step(row_item[0], row_item[1], gain_first, query_w, key_w, value_w, out_w, gain_second, gate_w, up_w, down_w))
        _, outputs = lax.scan(one_row, jnp.zeros((), jnp.float32), (all_tokens, lengths))
        return outputs
    layer_out, pull_back = jax.vjp(forward, tokens.astype(jnp.float32), gain_one.astype(jnp.float32), w_query.astype(jnp.float32), w_key.astype(jnp.float32), w_value.astype(jnp.float32), w_out.astype(jnp.float32), gain_two.astype(jnp.float32), w_gate.astype(jnp.float32), w_up.astype(jnp.float32), w_down.astype(jnp.float32))
    grads = pull_back(cotangent.astype(jnp.float32))
    return (layer_out, grads[0], grads[1], grads[2], grads[3], grads[4], grads[5], grads[6], grads[7], grads[8], grads[9])
```

```python
import functools

import jax
import jax.numpy as jnp
import numpy as np
from jax import lax
from jax.experimental import pallas as pl
from jax.experimental.pallas import tpu as pltpu
from jax.sharding import PartitionSpec as P

HEADS = 16
FDIM = 16
VHEAD = 128
EPS = 1e-06

bf16 = jnp.bfloat16
f32 = jnp.float32

PAIRS = [(a, b) for a in range(FDIM + 1) for b in range(a, FDIM + 1)]
NPAIR = len(PAIRS)
PADF = 256
STATE_ROWS = 160
CONST = 1 << 20

NN = (((1,), (0,)), ((), ()))
NT = (((1,), (1,)), ((), ()))
TN = (((0,), (0,)), ((), ()))


def mm(a, b, dims=NN):
    return lax.dot_general(a, b, dims, preferred_element_type=f32)


def feature_tables():
    index = np.full((8, PADF), -CONST, np.int32)
    level = np.zeros((8, PADF), np.float32)
    for f, (a, b) in enumerate(PAIRS):
        index[0, f] = a if a < FDIM else CONST
        index[1, f] = b if b < FDIM else CONST
        level[0, f] = float(a == FDIM)
        level[1, f] = float(b == FDIM)
        if a == FDIM:
            level[2, f] = 1.0
        elif b == FDIM:
            level[2, f] = FDIM**-0.5
        elif a == b:
            level[2, f] = 1.0 / (2 * FDIM)
        else:
            level[2, f] = 1.0 / FDIM
    return jnp.asarray(index), jnp.asarray(level)


def cost(flops, moved, trans=0):
    return pl.CostEstimate(flops=int(flops), bytes_accessed=int(moved), transcendentals=int(trans))


def params(mib):
    return pltpu.CompilerParams(vmem_limit_bytes=mib << 20)


def selectors(head, index):
    lanes = lax.broadcasted_iota(jnp.int32, (HEADS * FDIM, PADF), 0) - FDIM * head
    pick_a = jnp.where(lanes == index[0:1, :], 1.0, 0.0).astype(bf16)
    pick_b = jnp.where(lanes == index[1:2, :], 1.0, 0.0).astype(bf16)
    return pick_a, pick_b


def factors(packed, pick_a, pick_b, level):
    return mm(packed, pick_a) + level[0:1, :], mm(packed, pick_b) + level[1:2, :]


def own_lanes(head, packed):
    lane = lax.broadcasted_iota(jnp.int32, packed.shape, 1)
    return jnp.where(lane // FDIM == head, packed, jnp.zeros_like(packed))


def pack_state(state, sums):
    block = state[:STATE_ROWS]
    high = sums.astype(bf16).astype(f32)
    low = sums - high
    row = lax.broadcasted_iota(jnp.int32, block.shape, 0)
    for k, part in enumerate((high[:, :128], high[:, 128:], low[:, :128], low[:, 128:])):
        block = jnp.where(row == NPAIR + k, part, block)
    return block.astype(bf16)


def unpack_state(block):
    row = lax.broadcasted_iota(jnp.int32, block.shape, 0)

    def line(k):
        return jnp.sum(jnp.where(row == NPAIR + k, block, 0.0), axis=0, keepdims=True)

    sums = jnp.concatenate([line(0) + line(2), line(1) + line(3)], axis=1)
    state = jnp.where(row < NPAIR, block, 0.0).astype(bf16)
    pad = jnp.zeros((PADF - STATE_ROWS, VHEAD), bf16)
    return jnp.concatenate([state, pad], axis=0), sums


def column(ref, head):
    lane = lax.broadcasted_iota(jnp.int32, ref.shape, 1)
    return jnp.sum(jnp.where(lane == head, ref[...], 0.0), axis=1, keepdims=True)


def key_state_kernel(index, level, k_ref, v_ref, end_ref, out_ref):
    head = pl.program_id(0)
    pick_a, pick_b = selectors(head, index)
    one, two = factors(k_ref[...], pick_a, pick_b, level)
    feats = (one * two * end_ref[:, 0:1]).astype(bf16)
    state = mm(feats, v_ref[...], TN)
    sums = jnp.sum(feats.astype(f32), axis=0, keepdims=True)
    out_ref[0] = pack_state(state, sums)


def intra_kernel(q_ref, k_ref, v_ref, mask_ref, num_ref, den_ref):
    head = pl.program_id(0)
    scores = mm(own_lanes(head, q_ref[...]), k_ref[...], NT)
    lin = scores * 0.25 + 1.0
    weights = ((lin * lin * 0.5 + 0.5) * mask_ref[...]).astype(bf16)
    values = v_ref[...]
    both = mm(weights, jnp.concatenate([values, jnp.ones_like(values)], axis=1))
    num_ref[...] = both[:, :VHEAD]
    lane = lax.broadcasted_iota(jnp.int32, den_ref.shape, 1)

    @pl.when(head == 0)
    def _():
        den_ref[...] = jnp.zeros_like(den_ref)

    den_ref[...] = jnp.where(lane == head, both[:, VHEAD:], den_ref[...])


def combine_kernel(index, level, q_ref, num_ref, den_ref, state_ref, from_ref, mixed_ref, total_ref):
    head = pl.program_id(0)
    pick_a, pick_b = selectors(head, index)
    one, two = factors(q_ref[...], pick_a, pick_b, level)
    feats = (one * two * level[2:3, :]).astype(bf16)
    state, sums = unpack_state(state_ref[0])
    reach = from_ref[:, 0:1]
    carried = mm(feats, state)
    carried_den = jnp.sum(feats.astype(f32) * sums, axis=1, keepdims=True)
    den = column(den_ref, head) + reach * carried_den
    mixed_ref[...] = ((num_ref[...] + reach * carried) / den).astype(bf16)
    lane = lax.broadcasted_iota(jnp.int32, total_ref.shape, 1)

    @pl.when(head == 0)
    def _():
        total_ref[...] = jnp.zeros_like(total_ref)

    total_ref[...] = jnp.where(lane == head, den, total_ref[...])


def query_state_kernel(
    index, level, q_ref, grad_ref, mixed_ref, den_ref, from_ref, out_ref, gnum_ref, gden_ref
):
    head = pl.program_id(0)
    pick_a, pick_b = selectors(head, index)
    one, two = factors(q_ref[...], pick_a, pick_b, level)
    feats = (one * two * level[2:3, :]).astype(bf16)
    gnum = (grad_ref[...] / column(den_ref, head)).astype(bf16)
    wide = gnum.astype(f32)
    gden = -jnp.sum(wide * mixed_ref[...].astype(f32), axis=1, keepdims=True)
    reach = from_ref[:, 0:1]
    state = mm(feats, (wide * reach).astype(bf16), TN)
    sums = jnp.sum(feats.astype(f32) * (gden * reach), axis=0, keepdims=True)
    out_ref[0] = pack_state(state, sums)
    gnum_ref[...] = gnum
    lane = lax.broadcasted_iota(jnp.int32, gden_ref.shape, 1)

    @pl.when(head == 0)
    def _():
        gden_ref[...] = jnp.zeros_like(gden_ref)

    gden_ref[...] = jnp.where(lane == head, gden, gden_ref[...])


def back_kernel(
    index,
    level,
    q_ref,
    k_ref,
    v_ref,
    mask_ref,
    gnum_ref,
    gden_ref,
    state_ref,
    from_ref,
    gq_ref,
    gk_ref,
    gv_ref,
    gq_sum,
):
    head = pl.program_id(0)
    queries, keys, values = q_ref[...], k_ref[...], v_ref[...]
    gnum = gnum_ref[...]
    gden = column(gden_ref, head)
    q_own, k_own = own_lanes(head, queries), own_lanes(head, keys)
    scores = mm(q_own, keys, NT)
    lin = scores * 0.25 + 1.0
    mask = mask_ref[...]
    weights = ((lin * lin * 0.5 + 0.5) * mask).astype(bf16)
    slopes = ((mm(gnum, values, NT) + gden) * (mask * lin * 0.25)).astype(bf16)
    gv_ref[...] = mm(weights, gnum, TN)
    grad_q = mm(slopes, k_own)
    grad_k = mm(slopes, q_own, TN)

    pick_a, pick_b = selectors(head, index)
    one, two = factors(queries, pick_a, pick_b, level)
    state, sums = unpack_state(state_ref[0])
    gfeat = (mm(gnum, state, NT) + gden * sums) * from_ref[:, 0:1] * level[2:3, :]
    grad_q += mm((gfeat * two).astype(bf16), pick_a, NT)
    grad_q += mm((gfeat * one).astype(bf16), pick_b, NT)

    @pl.when(head == 0)
    def _():
        gq_sum[...] = jnp.zeros_like(gq_sum)
        gk_ref[...] = jnp.zeros_like(gk_ref)

    gq_sum[...] += grad_q
    gk_ref[...] += grad_k

    @pl.when(head == HEADS - 1)
    def _():
        gq_ref[...] = gq_sum[...].astype(bf16)


def back_state_kernel(
    index, level, k_ref, v_ref, gstate_ref, end_ref, gk_in, gv_in, gk_ref, gv_ref, gk_sum
):
    head = pl.program_id(0)
    values = v_ref[...]
    pick_a, pick_b = selectors(head, index)
    one, two = factors(k_ref[...], pick_a, pick_b, level)
    state, sums = unpack_state(gstate_ref[0])
    reach = end_ref[:, 0:1]
    feats = (one * two * reach).astype(bf16)
    gv_ref[...] = (gv_in[...] + mm(feats, state)).astype(bf16)
    gfeat = (mm(values, state, NT) + sums) * reach
    grad_k = mm((gfeat * two).astype(bf16), pick_a, NT)
    grad_k += mm((gfeat * one).astype(bf16), pick_b, NT)

    @pl.when(head == 0)
    def _():
        gk_sum[...] = gk_in[...]

    gk_sum[...] += grad_k

    @pl.when(head == HEADS - 1)
    def _():
        gk_ref[...] = gk_sum[...].astype(bf16)


def whole(shape):
    return pl.BlockSpec(shape, lambda h: (0,) * len(shape))


def per_head(length):
    return pl.BlockSpec((length, VHEAD), lambda h: (0, h))


STATE_SPEC = pl.BlockSpec((1, STATE_ROWS, VHEAD), lambda h: (h, 0, 0))


def head_call(kernel, tables, operands, in_specs, out_shape, out_specs, scratch, flops, moved):
    if tables is not None:

        def body(index_ref, level_ref, *refs):
            kernel(index_ref[...], level_ref[...], *refs)

        operands = (*tables, *operands)
        in_specs = [whole((8, PADF)), whole((8, PADF)), *in_specs]
    else:
        body = kernel
    return pl.pallas_call(
        body,
        grid=(HEADS,),
        in_specs=in_specs,
        out_specs=out_specs,
        out_shape=out_shape,
        scratch_shapes=scratch,
        compiler_params=params(40),
        cost_estimate=cost(flops, moved),
    )(*operands)


def sds(shape, dtype):
    return jax.ShapeDtypeStruct(shape, dtype)


def ff_act_kernel(half, which_ref, x0, x1, g0, g1, wg, wu, wd, hid, gg, gu):
    step = pl.program_id(0)
    first = step < half
    tokens = jnp.where(first, x0[...], x1[...])
    branch = jnp.where(first, g0[...], g1[...])
    gate = mm(tokens, wg[...])
    up = mm(tokens, wu[...])
    grad = mm(branch, wd[...], NT)
    sig = 1.0 / (1.0 + jnp.exp(-gate))
    silu = gate * sig
    hid[...] = (silu * up).astype(bf16)
    gg[...] = (grad * up * (sig * (1.0 + gate * (1.0 - sig)))).astype(bf16)
    gu[...] = (grad * silu).astype(bf16)


def ff_out_kernel(half, which_ref, hid, gg, gu, wg, wu, wd, low0, low1, lay0, lay1):
    step = pl.program_id(0)
    low = (mm(gg[...], wg[...], NT) + mm(gu[...], wu[...], NT)).astype(bf16)
    lay = mm(hid[...], wd[...]).astype(bf16)

    @pl.when(step < half)
    def _():
        low0[...] = low
        lay0[...] = lay

    @pl.when(step >= half)
    def _():
        low1[...] = low
        lay1[...] = lay


def ff_specs(width, slice_ff):
    once = pl.Buffered(1)
    return [
        pl.BlockSpec((width, slice_ff), lambda i, w: (0, w[0]), pipeline_mode=once),
        pl.BlockSpec((width, slice_ff), lambda i, w: (0, w[0]), pipeline_mode=once),
        pl.BlockSpec((slice_ff, width), lambda i, w: (w[0], 0), pipeline_mode=once),
    ]


def ff_act(which, x0, x1, g0, g1, wg, wu, wd, slice_ff):
    count, width = x0.shape
    tile = min(256, count)
    half = count // tile
    low = pl.BlockSpec((tile, width), lambda i, w: (jnp.minimum(i, half - 1), 0))
    high = pl.BlockSpec((tile, width), lambda i, w: (jnp.maximum(i - half, 0), 0))
    out = pl.BlockSpec((tile, slice_ff), lambda i, w: (i, 0))
    total = 2 * count
    return pl.pallas_call(
        functools.partial(ff_act_kernel, half),
        grid_spec=pltpu.PrefetchScalarGridSpec(
            num_scalar_prefetch=1,
            grid=(2 * half,),
            in_specs=[low, high, low, high, *ff_specs(width, slice_ff)],
            out_specs=[out, out, out],
        ),
        out_shape=[sds((total, slice_ff), bf16)] * 3,
        compiler_params=params(56),
        cost_estimate=cost(
            6 * total * width * slice_ff,
            6 * width * slice_ff + 4 * total * width + 6 * total * slice_ff,
            2 * total * slice_ff,
        ),
    )(which, x0, x1, g0, g1, wg, wu, wd)


def ff_out(which, hid, gg, gu, wg, wu, wd, slice_ff):
    total, width = hid.shape[0], wg.shape[0]
    count = total // 2
    tile = min(256, count)
    half = count // tile
    row = pl.BlockSpec((tile, slice_ff), lambda i, w: (i, 0))
    low = pl.BlockSpec((tile, width), lambda i, w: (jnp.minimum(i, half - 1), 0))
    high = pl.BlockSpec((tile, width), lambda i, w: (jnp.maximum(i - half, 0), 0))
    return pl.pallas_call(
        functools.partial(ff_out_kernel, half),
        grid_spec=pltpu.PrefetchScalarGridSpec(
            num_scalar_prefetch=1,
            grid=(2 * half,),
            in_specs=[row, row, row, *ff_specs(width, slice_ff)],
            out_specs=[low, high, low, high],
        ),
        out_shape=[sds((count, width), bf16)] * 4,
        compiler_params=params(56),
        cost_estimate=cost(
            6 * total * width * slice_ff,
            6 * width * slice_ff + 4 * total * width + 6 * total * slice_ff,
        ),
    )(which, hid, gg, gu, wg, wu, wd)


def wide_grad_kernel(groups, ybit_ref, l0, l1, l2, l3, near, far, send, keep):
    count = l0.shape[0]
    total = mm(l0[...], near[:count, :], TN)
    total += mm(l1[...], near[count:, :], TN)
    total += mm(l2[...], far[:count, :], TN)
    total += mm(l3[...], far[count:, :], TN)
    rows = total.shape[0] // groups
    high = ybit_ref[0] == 1
    for g in range(groups):
        a = total[g * rows : g * rows + rows // 2]
        b = total[g * rows + rows // 2 : (g + 1) * rows]
        send[g] = jnp.where(high, a, b).astype(bf16)
        keep[g] = jnp.where(high, b, a).astype(bf16)


def wide_grad(ybit, lows, near, far, group_rows):
    count, width = lows[0].shape
    cols = near.shape[1]
    tile = min(256, width)
    groups = tile // group_rows
    lane = pl.BlockSpec((count, tile), lambda i, w: (0, i))
    held = pl.BlockSpec((2 * count, cols), lambda i, w: (0, 0), pipeline_mode=pl.Buffered(1))
    out = pl.BlockSpec((groups, group_rows // 2, cols), lambda i, w: (i, 0, 0))
    shape = sds((width // group_rows, group_rows // 2, cols), bf16)
    return pl.pallas_call(
        functools.partial(wide_grad_kernel, groups),
        grid_spec=pltpu.PrefetchScalarGridSpec(
            num_scalar_prefetch=1,
            grid=(width // tile,),
            in_specs=[lane, lane, lane, lane, held, held],
            out_specs=[out, out],
        ),
        out_shape=[shape, shape],
        compiler_params=params(48),
        cost_estimate=cost(
            8 * count * width * cols, 8 * count * (width + cols) + 2 * width * cols
        ),
    )(ybit, *lows, near, far)


def down_grad_kernel(near, far, g0, g1, g2, g3, out):
    count = g0.shape[0]
    total = mm(near[:count, :], g0[...], TN)
    total += mm(near[count:, :], g1[...], TN)
    total += mm(far[:count, :], g2[...], TN)
    total += mm(far[count:, :], g3[...], TN)
    out[...] = total.astype(bf16)


def down_grad(near, far, grads):
    count, width = grads[0].shape
    rows = near.shape[1]
    tile = min(256, width)
    lane = pl.BlockSpec((count, tile), lambda i: (0, i))
    held = pl.BlockSpec((2 * count, rows), lambda i: (0, 0), pipeline_mode=pl.Buffered(1))
    return pl.pallas_call(
        down_grad_kernel,
        grid=(width // tile,),
        in_specs=[held, held, lane, lane, lane, lane],
        out_specs=pl.BlockSpec((rows, tile), lambda i: (0, i)),
        out_shape=sds((rows, width), bf16),
        compiler_params=params(48),
        cost_estimate=cost(
            8 * count * width * rows, 8 * count * (width + rows) + 2 * width * rows
        ),
    )(near, far, *grads)


def total_of(terms):
    total = terms[0].astype(f32)
    for term in terms[1:]:
        total = total + term.astype(f32)
    return total


def take(terms, dim, place):
    return [lax.dynamic_index_in_dim(t, place, dim, keepdims=False) for t in terms]


def pair_sum(terms, dim, bit, swap, kind=bf16):
    sent = total_of(take(terms, dim, 1 - bit)).astype(kind)
    return [*take(terms, dim, bit), swap(sent)]


def ring_sum(pick, seq, length, kind=bf16):
    ring = [(s, (s + 1) % length) for s in range(length)]
    held = None
    for k in range(length - 1):
        block = lax.rem(seq - 1 - k + 2 * length, length)
        terms = pick(block) + ([held] if held is not None else [])
        held = lax.ppermute(total_of(terms).astype(kind), "seq", ring)
    return pick(seq) + [held]


def shards(
    tokens,
    lengths,
    gain_one,
    w_query,
    w_key,
    w_value,
    w_out,
    gain_two,
    w_gate,
    w_up,
    w_down,
    cotangent,
):
    rows_dev, stretch, width = tokens.shape
    nfeat, nseq, nrows = (lax.axis_size(a) for a in ("feat", "seq", "rows"))
    assert rows_dev == 1 and nfeat == 2 and nrows == 4 and nseq % 2 == 0
    ff = w_gate.shape[1]
    fi, si, ri = (lax.axis_index(a) for a in ("feat", "seq", "rows"))
    xb, yb = ri % 2, ri // 2
    slice_ff = ff // 4
    which = jnp.reshape(2 * fi + xb, (1,)).astype(jnp.int32)
    ybit = jnp.reshape(yb, (1,)).astype(jnp.int32)

    def over_feat(a):
        return lax.ppermute(a, "feat", [(0, 1), (1, 0)])

    def over_x(a):
        return lax.ppermute(a, "rows", [(r, r ^ 1) for r in range(nrows)])

    def over_y(a):
        return lax.ppermute(a, "rows", [(r, r ^ 2) for r in range(nrows)])

    def spread(own):
        near = over_feat(own)
        far = over_x(own)
        return near, far, over_feat(far)

    flat = tokens.reshape(stretch, width)
    seed = cotangent.reshape(stretch, width)
    grad_branch = lax.optimization_barrier(seed.astype(bf16))
    branch1, branch2, branch3 = spread(grad_branch)

    ndocs = lengths.shape[1]
    doc_lengths = lax.dynamic_index_in_dim(lengths, fi * nrows + ri, 0, keepdims=False)
    starts = jnp.cumsum(doc_lengths) - doc_lengths
    offset = si * stretch

    def doc_of(places):
        return jnp.sum((starts[None, :] <= places[:, None]).astype(jnp.int32), axis=1)

    places = offset + jnp.arange(stretch, dtype=jnp.int32)
    docs = doc_of(places)
    hops = jnp.arange(1, nseq, dtype=jnp.int32)
    before = doc_of(jnp.reshape(offset - 1, (1,)))
    final = doc_of(jnp.reshape(offset + stretch - 1, (1,)))
    causal = jnp.arange(stretch)[None, :] <= jnp.arange(stretch)[:, None]
    mask = ((docs[:, None] == docs[None, :]) & causal).astype(f32)
    from_before = jnp.broadcast_to((docs == before).astype(f32)[:, None], (stretch, 128))
    at_end = jnp.broadcast_to((docs == final).astype(f32)[:, None], (stretch, 128))
    earlier = (doc_of(offset - 1 - (hops - 1) * stretch) == before).astype(f32)
    later = (doc_of(offset + hops * stretch - 1) == final).astype(f32)

    tables = feature_tables()
    length_spec = whole((stretch, 128))
    pack_spec = whole((stretch, HEADS * FDIM))
    mask_spec = whole((stretch, stretch))
    head_spec = per_head(stretch)
    state_shape = sds((HEADS, STATE_ROWS, VHEAD), bf16)
    unit = 2 * HEADS * stretch * 256

    def carried(state, shift, kept):
        pairs = [(s, s + shift) for s in range(nseq) if 0 <= s + shift < nseq]
        total = jnp.zeros(state.shape, f32)
        for k in range(nseq - 1):
            state = lax.ppermute(state, "seq", pairs)
            total = total + kept[k] * state.astype(f32)
        return total

    root_one = lax.rsqrt(jnp.mean(flat * flat, axis=-1, keepdims=True) + EPS)
    low_one = (flat * root_one * gain_one).astype(bf16)
    keys = mm(low_one, w_key).astype(bf16)
    values = mm(low_one, w_value).astype(bf16)
    queries = mm(low_one, w_query).astype(bf16)

    key_state = head_call(
        key_state_kernel,
        tables,
        (keys, values, at_end),
        [pack_spec, head_spec, length_spec],
        state_shape,
        STATE_SPEC,
        [],
        unit * 3 * 256,
        4 << 20,
    )
    state_in = carried(key_state, 1, earlier)
    numer, denom_here = head_call(
        intra_kernel,
        None,
        (queries, keys, values, mask),
        [pack_spec, pack_spec, head_spec, mask_spec],
        [sds((stretch, width), f32), sds((stretch, 128), f32)],
        [head_spec, length_spec],
        [],
        unit * 4 * 256,
        9 << 20,
    )
    mixed_low, denom = head_call(
        combine_kernel,
        tables,
        (queries, numer, denom_here, state_in, from_before),
        [pack_spec, head_spec, length_spec, STATE_SPEC, length_spec],
        [sds((stretch, width), bf16), sds((stretch, 128), f32)],
        [head_spec, length_spec],
        [],
        unit * 3 * 256,
        9 << 20,
    )
    middle = flat + mm(mixed_low, w_out)
    root_two = lax.rsqrt(jnp.mean(middle * middle, axis=-1, keepdims=True) + EPS)
    low_two = lax.optimization_barrier((middle * root_two * gain_two).astype(bf16))
    low1, low2, low3 = spread(low_two)

    weights = (w_gate, w_up, w_down)
    hid_n, gg_n, gu_n = ff_act(
        which, low_two, low1, grad_branch, branch1, *weights, slice_ff
    )
    glow0, glow1, lay0, lay1 = ff_out(which, hid_n, gg_n, gu_n, *weights, slice_ff)
    hid_f, gg_f, gu_f = ff_act(which, low2, low3, branch2, branch3, *weights, slice_ff)
    glow2, glow3, lay2, lay3 = ff_out(which, hid_f, gg_f, gu_f, *weights, slice_ff)

    def gathered(own, near, far, far_near):
        other = (far.astype(f32) + over_feat(far_near).astype(f32)).astype(bf16)
        return total_of([own, over_feat(near), over_x(other)])

    grad_low_two = gathered(glow0, glow1, glow2, glow3)
    lay_sum = gathered(lay0, lay1, lay2, lay3)
    layer_out = middle + lay_sum

    lows = (low_two, low1, low2, low3)
    group_rows = width // (2 * nseq)

    def wide_share(near, far):
        sent, kept = wide_grad(ybit, lows, near, far, group_rows)
        terms = [kept, over_y(sent)]
        split = [t.reshape(2, nseq, 2, group_rows // 4, slice_ff) for t in terms]
        mine = total_of(ring_sum(lambda b: take(split, 1, b), si, nseq)).astype(bf16)
        own = lax.dynamic_index_in_dim(mine, xb, 1, keepdims=False)
        other = over_x(lax.dynamic_index_in_dim(mine, 1 - xb, 1, keepdims=False))
        cols = jnp.where(
            xb == 0,
            jnp.concatenate([own, other], axis=-1),
            jnp.concatenate([other, own], axis=-1),
        )
        own = lax.dynamic_index_in_dim(cols, fi, 0, keepdims=False)
        other = over_feat(lax.dynamic_index_in_dim(cols, 1 - fi, 0, keepdims=False))
        return jnp.where(
            fi == 0,
            jnp.concatenate([own, other], axis=-1),
            jnp.concatenate([other, own], axis=-1),
        ).astype(f32)

    def down_share():
        grad = down_grad(hid_n, hid_f, (grad_branch, branch1, branch2, branch3))
        rows = slice_ff // (2 * nseq)
        split = grad.reshape(nseq // 2, 2, 2, rows, width)

        def pick(b):
            zero = jnp.int32(0)
            part = lax.dynamic_slice(
                split,
                (b % (nseq // 2), zero, b // (nseq // 2), zero, zero),
                (1, 2, 1, rows, width),
            )
            return [part.reshape(2, rows, width)]

        terms = ring_sum(pick, si, nseq)
        terms = pair_sum(terms, 0, yb, over_y)
        mine = total_of(terms).astype(bf16)
        swaps = []
        for s in range(nseq):
            for r in range(nrows):
                x = s // (nseq // 2)
                if x != r % 2:
                    to = (r % 2) * (nseq // 2) + s % (nseq // 2)
                    swaps.append((s * nrows + r, to * nrows + (r ^ 1)))
        moved = lax.ppermute(mine, ("seq", "rows"), swaps)
        stays = (si // (nseq // 2)) == xb
        return jnp.where(stays, mine, moved).astype(f32)

    grad_gate_w = wide_share(gg_n, gg_f)
    grad_up_w = wide_share(gu_n, gu_f)
    grad_down_w = down_share()

    unit_two = middle * root_two
    grad_gain_two = jnp.sum(grad_low_two * unit_two, axis=0)
    scaled = grad_low_two * gain_two
    grad_middle = seed + root_two * (
        scaled - unit_two * jnp.mean(scaled * unit_two, axis=-1, keepdims=True)
    )
    grad_mixed_low = grad_middle.astype(bf16)
    grad_mixed = mm(grad_mixed_low, w_out, NT)

    query_state, gnum, gden = head_call(
        query_state_kernel,
        tables,
        (queries, grad_mixed, mixed_low, denom, from_before),
        [pack_spec, head_spec, head_spec, length_spec, length_spec],
        [state_shape, sds((stretch, width), bf16), sds((stretch, 128), f32)],
        [STATE_SPEC, head_spec, length_spec],
        [],
        unit * 3 * 256,
        10 << 20,
    )
    state_back = carried(query_state, -1, later)
    grad_queries, grad_keys_part, grad_values_part = head_call(
        back_kernel,
        tables,
        (queries, keys, values, mask, gnum, gden, state_in, from_before),
        [
            pack_spec,
            pack_spec,
            head_spec,
            mask_spec,
            head_spec,
            length_spec,
            STATE_SPEC,
            length_spec,
        ],
        [
            sds((stretch, HEADS * FDIM), bf16),
            sds((stretch, HEADS * FDIM), f32),
            sds((stretch, width), f32),
        ],
        [pack_spec, pack_spec, head_spec],
        [pltpu.VMEM((stretch, HEADS * FDIM), f32)],
        unit * 15 * 256,
        10 << 20,
    )
    grad_keys, grad_values_low = head_call(
        back_state_kernel,
        tables,
        (keys, values, state_back, at_end, grad_keys_part, grad_values_part),
        [pack_spec, head_spec, STATE_SPEC, length_spec, pack_spec, head_spec],
        [sds((stretch, HEADS * FDIM), bf16), sds((stretch, width), bf16)],
        [pack_spec, head_spec],
        [pltpu.VMEM((stretch, HEADS * FDIM), f32)],
        unit * 6 * 256,
        10 << 20,
    )
    grad_low_one = (
        mm(grad_queries, w_query, NT)
        + mm(grad_keys, w_key, NT)
        + mm(grad_values_low, w_value, NT)
    )
    unit_one = flat * root_one
    grad_gain_one = jnp.sum(grad_low_one * unit_one, axis=0)
    scaled = grad_low_one * gain_one
    grad_tokens = grad_middle + root_one * (
        scaled - unit_one * jnp.mean(scaled * unit_one, axis=-1, keepdims=True)
    )

    part = width // (8 * nseq)

    def share(grad, order, kind=bf16):
        terms = [grad.reshape(2, nseq, 2, 2, part, grad.shape[-1])]
        dims = {"feat": 0, "seq": 1, "y": 2, "x": 3}
        for name in order:
            dim = dims.pop(name)
            dims = {k: v - (v > dim) for k, v in dims.items()}
            if name == "seq":
                now = terms
                terms = ring_sum(lambda b: take(now, dim, b), si, nseq, kind)
            else:
                bit, swap = {
                    "feat": (fi, over_feat),
                    "x": (xb, over_x),
                    "y": (yb, over_y),
                }[name]
                terms = pair_sum(terms, dim, bit, swap, kind)
        return total_of(terms)

    grad_out_w = share(mm(mixed_low, grad_mixed_low, TN).astype(bf16), ("feat", "x", "y", "seq"))
    grad_value_w = share(
        mm(low_one, grad_values_low, TN).astype(bf16), ("feat", "x", "y", "seq")
    )
    grad_qk = mm(low_one, jnp.concatenate([grad_queries, grad_keys], axis=-1), TN).astype(bf16)
    grad_qk_w = share(grad_qk, ("feat", "x", "seq", "y"))
    both = jnp.concatenate(
        [grad_gain_one.reshape(-1, 1, part), grad_gain_two.reshape(-1, 1, part)], axis=-1
    )
    blocks = [both.reshape(2, nseq, 2, 2, 2 * part)]
    blocks = pair_sum(blocks, 0, fi, over_feat, f32)
    blocks = pair_sum(blocks, 1, yb, over_y, f32)
    blocks = pair_sum(blocks, 1, xb, over_x, f32)
    now = blocks
    gains = total_of(ring_sum(lambda b: take(now, 0, b), si, nseq, f32))

    qk = w_query.shape[1]
    return (
        layer_out.reshape(rows_dev, stretch, width),
        grad_tokens.reshape(rows_dev, stretch, width),
        gains[:part],
        grad_qk_w[:, :qk],
        grad_qk_w[:, qk:],
        grad_value_w,
        grad_out_w,
        gains[part:],
        grad_gate_w,
        grad_up_w,
        grad_down_w,
    )


def solution(mesh):
    split = P(("feat", "rows"), "seq", None)
    vector = P(("feat", "seq", "rows"))
    matrix = P(("feat", "seq", "rows"), None)
    in_specs = (split, *(P() for _ in range(10)), split)
    out_specs = (
        split,
        split,
        vector,
        matrix,
        matrix,
        matrix,
        matrix,
        vector,
        matrix,
        matrix,
        matrix,
    )
    return jax.shard_map(shards, mesh=mesh, in_specs=in_specs, out_specs=out_specs, check_vma=False)
```

```python
import functools

import jax
import jax.numpy as jnp
import ml_dtypes
import numpy as np
from jax import lax
from jax.experimental import pallas as pl
from jax.experimental.pallas import tpu as pltpu
from jax.sharding import PartitionSpec as P

HEADS = 16
FDIM = 16
VHEAD = 128
EPS = 1e-06

bf16 = jnp.bfloat16
f32 = jnp.float32

PAIRS = [(a, b) for a in range(FDIM + 1) for b in range(a, FDIM + 1)]
NPAIR = len(PAIRS)
PADF = 256
STATE_ROWS = 160
VMEM_MIB = 30
bf16 = jnp.bfloat16
f32 = jnp.float32

PAIRS = [(a, b) for a in range(FDIM + 1) for b in range(a, FDIM + 1)]
NPAIR = len(PAIRS)
PADF = 256
STATE_ROWS = 160
VMEM_MIB = 30
SCALE = 20

NN = (((1,), (0,)), ((), ()))
NT = (((1,), (1,)), ((), ()))
TN = (((0,), (0,)), ((), ()))


def mm(a, b, dims=NN):
    return lax.dot_general(a, b, dims, preferred_element_type=f32)


def feature_tables():
    level = np.zeros((8, PADF), np.float32)
    for f, (a, b) in enumerate(PAIRS):
        level[0, f] = float(a == FDIM)
        level[1, f] = float(b == FDIM)
        if a == FDIM:
            level[2, f] = 1.0
        elif b == FDIM:
            level[2, f] = FDIM**-0.5
        elif a == b:
            level[2, f] = 1.0 / (2 * FDIM)
        else:
            level[2, f] = 1.0 / FDIM
    pick = np.zeros((2, HEADS, HEADS * FDIM, PADF), np.float32)
    for head in range(HEADS):
        for f, pair in enumerate(PAIRS):
            for k, entry in enumerate(pair):
                if entry < FDIM:
                    pick[k, head, head * FDIM + entry, f] = 1.0
    pick = pick.astype(ml_dtypes.bfloat16)
    return jnp.asarray(pick[0]), jnp.asarray(pick[1]), jnp.asarray(level)


FREE = pl.CostEstimate(flops=0, bytes_accessed=0, transcendentals=0)


def params(mib):
    return pltpu.CompilerParams(vmem_limit_bytes=mib << 20)


def factors(packed, pick_a, pick_b, level):
    return mm(packed, pick_a[0]) + level[0:1, :], mm(packed, pick_b[0]) + level[1:2, :]


def wide(value, times):
    return jnp.concatenate([value] * times, axis=1)


def parts(value):
    high = value.astype(bf16)
    return high, (value - high.astype(f32)).astype(bf16)


def own_lanes(head, packed):
    lane = lax.broadcasted_iota(jnp.int32, packed.shape, 1)
    return jnp.where(lane // FDIM == head, packed, jnp.zeros_like(packed))


def pack_state(state, sums):
    block = state[:STATE_ROWS]
    high = sums.astype(bf16).astype(f32)
    low = sums - high
    row = lax.broadcasted_iota(jnp.int32, block.shape, 0)
    for k, part in enumerate((high[:, :128], high[:, 128:], low[:, :128], low[:, 128:])):
        block = jnp.where(row == NPAIR + k, part, block)
    return block.astype(bf16)


def unpack_state(block):
    row = lax.broadcasted_iota(jnp.int32, block.shape, 0)

    def line(k):
        return jnp.sum(jnp.where(row == NPAIR + k, block, 0.0), axis=0, keepdims=True)

    sums = jnp.concatenate([line(0) + line(2), line(1) + line(3)], axis=1)
    state = jnp.where(row < NPAIR, block, 0.0).astype(bf16)
    pad = jnp.zeros((PADF - STATE_ROWS, VHEAD), bf16)
    return jnp.concatenate([state, pad], axis=0), sums


def sum_against(feats, sums):
    return sum(mm(feats, p, NT) for p in parts(jnp.broadcast_to(sums, (128, PADF))))


def column(ref, head):
    row = lax.broadcasted_iota(jnp.int32, (128, 128), 0)
    pick = jnp.where(row == head, 1.0, 0.0).astype(bf16)
    return sum(mm(p, pick) for p in parts(ref[...]))


def row_sum(value):
    ones = jnp.ones((128, 128), bf16)
    return sum(mm(p, ones) for p in parts(value))


def set_column(ref, head, value):
    lane = lax.broadcasted_iota(jnp.int32, ref.shape, 1)

    @pl.when(head == 0)
    def _():
        ref[...] = jnp.zeros_like(ref)

    ref[...] = jnp.where(lane == head, value, ref[...])


def key_state_kernel(head, pick_a, pick_b, level, k_ref, v_ref, end_ref, out_ref):
    one, two = factors(k_ref[...], pick_a, pick_b, level)
    feats = (one * two * wide(end_ref[...], 2)).astype(bf16)
    state = mm(feats, v_ref[...], TN)
    sums = jnp.sum(feats.astype(f32), axis=0, keepdims=True)
    out_ref[0] = pack_state(state, sums)


def intra_kernel(head, pick_a, pick_b, level, q_ref, k_ref, v_ref, mask_ref, num_ref, den_ref, feat_ref):
    queries = q_ref[...]
    scores = mm(own_lanes(head, queries), k_ref[...], NT)
    lin = scores * 0.25 + 1.0
    weights = ((lin * lin * 0.5 + 0.5) * mask_ref[...]).astype(bf16)
    values = v_ref[...]
    both = mm(weights, jnp.concatenate([values, jnp.ones_like(values)], axis=1))
    num_ref[...] = both[:, :VHEAD]
    set_column(den_ref, head, both[:, VHEAD:])
    one, two = factors(queries, pick_a, pick_b, level)
    feat_ref[0] = (one * two * level[2:3, :]).astype(bf16)


def kept_state(kept_ref, state_refs):
    block = jnp.zeros(state_refs[0].shape[1:], f32)
    for k, ref in enumerate(state_refs):
        block = block + kept_ref[k] * ref[0].astype(f32)
    return block


def combine_kernel(head, kept_ref, feat_ref, num_ref, den_ref, from_ref, *refs):
    *state_refs, mixed_ref, total_ref, block_ref = refs
    feats = feat_ref[0]
    block = kept_state(kept_ref, state_refs)
    block_ref[0] = block
    state, sums = unpack_state(block)
    reach = from_ref[...]
    den = column(den_ref, head) + reach * sum_against(feats, sums)
    mixed_ref[...] = ((num_ref[...] + reach * mm(feats, state)) * (1.0 / den)).astype(bf16)
    set_column(total_ref, head, den)


def query_state_kernel(
    head, feat_ref, grad_ref, mixed_ref, den_ref, from_ref, out_ref, gnum_ref, gden_ref
):
    feats = feat_ref[0]
    gnum = (grad_ref[...] * (1.0 / column(den_ref, head))).astype(bf16)
    far = gnum.astype(f32)
    gden = -row_sum(far * mixed_ref[...].astype(f32))
    reach = from_ref[...]
    state = mm(feats, (far * reach).astype(bf16), TN)
    sums = jnp.sum(feats.astype(f32) * wide(gden * reach, 2), axis=0, keepdims=True)
    out_ref[0] = pack_state(state, sums)
    gnum_ref[...] = gnum
    set_column(gden_ref, head, gden)


def back_kernel(
    first,
    head,
    pick_a,
    pick_b,
    level,
    q_ref,
    k_ref,
    v_ref,
    mask_ref,
    gnum_ref,
    gden_ref,
    state_ref,
    from_ref,
    gq_in,
    gk_in,
    gv_in,
    gq_ref,
    gk_ref,
    gv_ref,
):
    queries, keys, values = q_ref[...], k_ref[...], v_ref[...]
    gnum = gnum_ref[...]
    gden = column(gden_ref, head)
    q_own, k_own = own_lanes(head, queries), own_lanes(head, keys)
    scores = mm(q_own, keys, NT)
    lin = scores * 0.25 + 1.0
    mask = mask_ref[...]
    weights = ((lin * lin * 0.5 + 0.5) * mask).astype(bf16)
    spread = wide(gden, keys.shape[0] // 128)
    slopes = ((mm(gnum, values, NT) + spread) * (mask * lin * 0.25)).astype(bf16)
    gv_ref[...] = mm(weights, gnum, TN)
    grad_q = mm(slopes, k_own)
    grad_k = mm(slopes, q_own, TN)

    one, two = factors(queries, pick_a, pick_b, level)
    state, sums = unpack_state(state_ref[0])
    reach = from_ref[...]
    gfeat = (mm(gnum, state, NT) + wide(gden, 2) * sums) * wide(reach, 2) * level[2:3, :]
    grad_q += mm((gfeat * two).astype(bf16), pick_a[0], NT)
    grad_q += mm((gfeat * one).astype(bf16), pick_b[0], NT)

    @pl.when(head == first)
    def _():
        if first == 0:
            gq_ref[...] = jnp.zeros_like(gq_ref)
            gk_ref[...] = jnp.zeros_like(gk_ref)
        else:
            gq_ref[...] = gq_in[...]
            gk_ref[...] = gk_in[...]

    gq_ref[...] += grad_q
    gk_ref[...] += grad_k


def back_state_kernel(
    head, kept_ref, pick_a, pick_b, level, k_ref, v_ref, end_ref, gk_in, gv_in, *refs
):
    *state_refs, gk_ref, gv_ref, gk_sum = refs
    values = v_ref[...]
    one, two = factors(k_ref[...], pick_a, pick_b, level)
    state, sums = unpack_state(kept_state(kept_ref, state_refs))
    reach = wide(end_ref[...], 2)
    feats = (one * two * reach).astype(bf16)
    gv_ref[...] = (gv_in[...] + mm(feats, state)).astype(bf16)
    gfeat = (mm(values, state, NT) + sums) * reach
    grad_k = mm((gfeat * two).astype(bf16), pick_a[0], NT)
    grad_k += mm((gfeat * one).astype(bf16), pick_b[0], NT)

    @pl.when(head == 0)
    def _():
        gk_sum[...] = gk_in[...]

    gk_sum[...] += grad_k

    @pl.when(head == HEADS - 1)
    def _():
        gk_ref[...] = gk_sum[...].astype(bf16)


def head_call(kernel, ins, outs, heads=(0, HEADS), scratch=(), aliases=None):
    first, last = heads

    def spec(kind, shape):
        if kind == "all":
            return pl.BlockSpec(shape, lambda h: (0,) * len(shape))
        if kind == "head":
            return pl.BlockSpec((shape[0], VHEAD), lambda h: (0, h + first))
        if kind == "state":
            return pl.BlockSpec((1, *shape[1:]), lambda h: (h + first, 0, 0))
        if kind == "smem":
            return pl.BlockSpec(memory_space=pltpu.SMEM)
        return pl.BlockSpec(memory_space=pl.ANY)

    def body(*refs):
        kernel(pl.program_id(0) + first, *refs)

    return pl.pallas_call(
        body,
        grid=(last - first,),
        in_specs=[spec(kind, a.shape) for kind, a in ins],
        out_specs=[spec(kind, shape) for kind, shape, _ in outs],
        out_shape=[sds(shape, dtype) for _, shape, dtype in outs],
        scratch_shapes=list(scratch),
        input_output_aliases=aliases or {},
        compiler_params=params(20),
        cost_estimate=FREE,
    )(*(a for _, a in ins))


def sds(shape, dtype):
    return jax.ShapeDtypeStruct(shape, dtype)


def hidden_grad_kernel(half, which_ref, g0, g1, wd, out):
    branch = jnp.where(pl.program_id(0) < half, g0[...], g1[...])
    out[...] = mm(branch, wd[...], NT).astype(bf16)


def act_kernel(half, which_ref, x0, x1, grad_ref, wg, wu, hid, gg, gu):
    tokens = jnp.where(pl.program_id(0) < half, x0[...], x1[...])
    gate = mm(tokens, wg[...])
    up = mm(tokens, wu[...])
    grad = grad_ref[...].astype(f32)
    sig = 1.0 / (1.0 + jnp.exp(-gate))
    silu = gate * sig
    hid[...] = (silu * up).astype(bf16)
    gg[...] = (grad * up * (sig * (1.0 + gate * (1.0 - sig)))).astype(bf16)
    gu[...] = (grad * silu).astype(bf16)


def put(half, value, low, pieces):
    step = pl.program_id(0)

    @pl.when(step < half)
    def _():
        low[...] = value

    for k, piece in enumerate(pieces):
        here = step == half + k if len(pieces) > 1 else step >= half

        @pl.when(here)
        def _(piece=piece):
            piece[...] = value


def low_grad_kernel(half, which_ref, gg, gu, wg, wu, low, *pieces):
    value = (mm(gg[...], wg[...], NT) + mm(gu[...], wu[...], NT)).astype(bf16)
    put(half, value, low, pieces)


def layer_kernel(half, which_ref, hid, wd, low, *pieces):
    put(half, mm(hid[...], wd[...]).astype(bf16), low, pieces)


def token_call(kernel, which, count, ins, outs, width, slice_ff):
    tile = min(256, count)
    half = count // tile
    once = pl.Buffered(1)
    low = pl.BlockSpec((tile, width), lambda i, w: (jnp.minimum(i, half - 1), 0))
    high = pl.BlockSpec((tile, width), lambda i, w: (jnp.maximum(i - half, 0), 0))
    row = pl.BlockSpec((tile, slice_ff), lambda i, w: (i, 0))
    specs, operands = [], []
    for kind, *arrays in ins:
        operands += arrays
        specs += {
            "pair": [low, high],
            "row": [row],
            "wide": [pl.BlockSpec((width, slice_ff), lambda i, w: (0, w[0]), pipeline_mode=once)],
            "tall": [pl.BlockSpec((slice_ff, width), lambda i, w: (w[0], 0), pipeline_mode=once)],
        }[kind]
    out_specs, out_shapes = [], []
    for kind in outs:
        if kind == "row":
            out_specs.append(row)
            out_shapes.append(sds((2 * count, slice_ff), bf16))
        elif kind == "two":
            out_specs += [low, high]
            out_shapes += [sds((count, width), bf16)] * 2
        else:
            piece = pl.BlockSpec((tile, width), lambda i, w: (0, 0))
            out_specs += [low] + [piece] * half
            out_shapes += [sds((count, width), bf16)] + [sds((tile, width), bf16)] * half
    return pl.pallas_call(
        functools.partial(kernel, half),
        grid_spec=pltpu.PrefetchScalarGridSpec(
            num_scalar_prefetch=1,
            grid=(2 * half,),
            in_specs=specs,
            out_specs=out_specs,
        ),
        out_shape=out_shapes,
        compiler_params=params(VMEM_MIB),
        cost_estimate=FREE,
    )(which, *operands)


def split_rows(total, high, send, keep):
    groups = send.shape[0]
    rows = total.shape[0] // groups
    for g in range(groups):
        a = total[g * rows : g * rows + rows // 2]
        b = total[g * rows + rows // 2 : (g + 1) * rows]
        send[g] = jnp.where(high, a, b).astype(bf16)
        keep[g] = jnp.where(high, b, a).astype(bf16)


def wide_grad_kernel(ybit_ref, l0, l1, l2, l3, near, far, send, keep):
    count = l0.shape[0]
    total = mm(l0[...], near[:count, :], TN)
    total += mm(l1[...], near[count:, :], TN)
    total += mm(l2[...], far[:count, :], TN)
    total += mm(l3[...], far[count:, :], TN)
    split_rows(total, ybit_ref[0] == 1, send, keep)


def wide_grad(ybit, lows, near, far, group_rows):
    count, width = lows[0].shape
    cols = near.shape[1]
    tile = min(256, width)
    groups = tile // group_rows
    lane = pl.BlockSpec((count, tile), lambda i, w: (0, i))
    held = pl.BlockSpec((2 * count, cols), lambda i, w: (0, 0), pipeline_mode=pl.Buffered(1))
    out = pl.BlockSpec((groups, group_rows // 2, cols), lambda i, w: (i, 0, 0))
    shape = sds((width // group_rows, group_rows // 2, cols), bf16)
    return pl.pallas_call(
        wide_grad_kernel,
        grid_spec=pltpu.PrefetchScalarGridSpec(
            num_scalar_prefetch=1,
            grid=(width // tile,),
            in_specs=[lane, lane, lane, lane, held, held],
            out_specs=[out, out],
        ),
        out_shape=[shape, shape],
        compiler_params=params(VMEM_MIB),
        cost_estimate=FREE,
    )(ybit, *lows, near, far)


def down_grad_kernel(ybit_ref, near, far, g0, g1, g2, g3, send, keep):
    count = g0.shape[0]
    total = mm(near[:count, :], g0[...], TN)
    total += mm(near[count:, :], g1[...], TN)
    total += mm(far[:count, :], g2[...], TN)
    total += mm(far[count:, :], g3[...], TN)
    split_rows(total, ybit_ref[0] == 1, send, keep)


def down_grad(ybit, near, far, grads, group_rows):
    count, width = grads[0].shape
    rows = near.shape[1]
    tile = min(256, width)
    lane = pl.BlockSpec((count, tile), lambda i, w: (0, i))
    held = pl.BlockSpec((2 * count, rows), lambda i, w: (0, 0), pipeline_mode=pl.Buffered(1))
    out = pl.BlockSpec((rows // group_rows, group_rows // 2, tile), lambda i, w: (0, 0, i))
    shape = sds((rows // group_rows, group_rows // 2, width), bf16)
    return pl.pallas_call(
        down_grad_kernel,
        grid_spec=pltpu.PrefetchScalarGridSpec(
            num_scalar_prefetch=1,
            grid=(width // tile,),
            in_specs=[held, held, lane, lane, lane, lane],
            out_specs=[out, out],
        ),
        out_shape=[shape, shape],
        compiler_params=params(VMEM_MIB),
        cost_estimate=FREE,
    )(ybit, near, far, *grads)


def norm_back_kernel(low, near, far, middle, seed, gain, w, grad_ref, low_ref, mixed_ref, gain_ref, *copies):
    grad = low[...].astype(f32) + near[...].astype(f32) + far[...].astype(f32)
    value = middle[...]
    root = lax.rsqrt(jnp.mean(value * value, axis=-1, keepdims=True) + EPS)
    unit = value * root

    @pl.when(pl.program_id(0) == 0)
    def _():
        gain_ref[...] = jnp.zeros_like(gain_ref)

    gain_ref[...] += jnp.broadcast_to(jnp.sum(grad * unit, axis=0, keepdims=True), gain_ref.shape)
    scaled = grad * gain[...]
    total = seed[...] + root * (scaled - unit * jnp.mean(scaled * unit, axis=-1, keepdims=True))
    grad_ref[...] = total
    narrow = total.astype(bf16)
    low_ref[...] = narrow
    for k, copy in enumerate(copies):

        @pl.when(pl.program_id(0) // 2 == k)
        def _(copy=copy):
            copy[...] = narrow

    mixed_ref[...] = mm(narrow, w[...], NT)


def norm_back(low, near, far, middle, seed, gain, w):
    count, width = middle.shape
    tile = min(128, count // 2)
    halves = count // (2 * tile)
    row = pl.BlockSpec((tile, width), lambda i: (i, 0))

    def held(shape):
        return pl.BlockSpec(shape, lambda i: (0, 0), pipeline_mode=pl.Buffered(1))

    return pl.pallas_call(
        norm_back_kernel,
        grid=(count // tile,),
        in_specs=[row] * 5 + [held((1, width)), held(w.shape)],
        out_specs=[row] * 3
        + [pl.BlockSpec((8, width), lambda i: (0, 0))]
        + [
            pl.BlockSpec((tile, width), lambda i, k=k: (jnp.clip(i - 2 * k, 0, 1), 0))
            for k in range(halves)
        ],
        out_shape=[
            sds((count, width), f32),
            sds((count, width), bf16),
            sds((count, width), f32),
            sds((8, width), f32),
            *[sds((2 * tile, width), bf16)] * halves,
        ],
        compiler_params=params(VMEM_MIB),
        cost_estimate=FREE,
    )(low, near, far, middle, seed, gain.reshape(1, width), w)


def core_grad_kernel(along_x, bits_ref, r0, r1, c0, *refs):
    *others, send, keep = refs
    total = mm(r0[...], c0[...], TN)
    first = 0
    for c1 in others:
        count = c1.shape[0]
        total += mm(r1[first : first + count, :], c1[...], TN)
        first += count
    groups, _, rows, _ = send.shape
    high = bits_ref[1 if along_x else 2] == 1
    for g in range(groups):

        def block(y, x):
            first = (4 * g + 2 * y + x) * rows
            return total[first : first + rows]

        for k in range(2):
            a, b = (block(k, 0), block(k, 1)) if along_x else (block(0, k), block(1, k))
            send[g, k] = jnp.where(high, a, b).astype(bf16)
            keep[g, k] = jnp.where(high, b, a).astype(bf16)


def core_grad(bits, r0, r1, c0, others, place, parts, nseq, along_x):
    count, width = r0.shape
    cols = c0.shape[1] // parts
    tile = min(256, width // 2)
    steps = width // 2 // tile
    rows = width // (8 * nseq)
    groups = tile // (4 * rows)
    lane = pl.BlockSpec((count, tile), lambda i, w: (0, w[0] * steps + i))

    def held(a):
        return pl.BlockSpec(
            (a.shape[0], cols), lambda i, w: (0, place), pipeline_mode=pl.Buffered(1)
        )

    out = pl.BlockSpec((groups, 2, rows, cols), lambda i, w: (i, 0, 0, 0))
    return pl.pallas_call(
        functools.partial(core_grad_kernel, along_x),
        grid_spec=pltpu.PrefetchScalarGridSpec(
            num_scalar_prefetch=1,
            grid=(steps,),
            in_specs=[lane, lane, held(c0), *(held(c) for c in others)],
            out_specs=[out, out],
        ),
        out_shape=[sds((nseq, 2, rows, cols), bf16)] * 2,
        compiler_params=params(VMEM_MIB),
        cost_estimate=FREE,
    )(bits, r0, r1, c0, *others)


def total_of(terms):
    total = terms[0].astype(f32)
    for term in terms[1:]:
        total = total + term.astype(f32)
    return total


def take(terms, dim, place):
    return [lax.dynamic_index_in_dim(t, place, dim, keepdims=False) for t in terms]


class Line:
    def __init__(self, mark):
        self.mark = mark

    def fence(self, *values):
        *values, self.mark = lax.optimization_barrier((*values, self.mark))
        return values[0] if len(values) == 1 else tuple(values)


class Task:
    def __init__(self, line, chain):
        self.line, self.chain, self.done = line, chain, False
        self.result = None
        self.waiting = next(chain)

    def step(self, count=1):
        for _ in range(count):
            if self.done:
                return
            try:
                self.waiting = self.chain.send(self.line.fence(self.waiting))
            except StopIteration as end:
                self.done, self.result = True, end.value

    def drain(self):
        while not self.done:
            self.step()
        return self.result


def shards(
    tokens,
    lengths,
    gain_one,
    w_query,
    w_key,
    w_value,
    w_out,
    gain_two,
    w_gate,
    w_up,
    w_down,
    cotangent,
):
    rows_dev, stretch, width = tokens.shape
    nfeat, nseq, nrows = (lax.axis_size(a) for a in ("feat", "seq", "rows"))
    assert rows_dev == 1 and nfeat == 2 and nrows == 4 and nseq % 2 == 0
    ff = w_gate.shape[1]
    fi, si, ri = (lax.axis_index(a) for a in ("feat", "seq", "rows"))
    xb, yb = ri % 2, ri // 2
    slice_ff = ff // 4
    which = jnp.reshape(2 * fi + xb, (1,)).astype(jnp.int32)
    ybit = jnp.reshape(yb, (1,)).astype(jnp.int32)
    bits = jnp.stack([fi, xb, yb]).astype(jnp.int32)

    line = Line((lengths[0, :1] < 0).astype(f32))
    fence = line.fence

    def over_feat(a):
        return lax.ppermute(a, "feat", [(0, 1), (1, 0)])

    def over_x(a):
        return lax.ppermute(a, "rows", [(r, r ^ 1) for r in range(nrows)])

    def over_y(a):
        return lax.ppermute(a, "rows", [(r, r ^ 2) for r in range(nrows)])

    def over_seq(a, shift=1):
        return lax.ppermute(a, "seq", [(s, (s + shift) % nseq) for s in range(nseq)])

    def hops(state):
        states = []
        for _ in range(nseq - 1):
            state = yield over_seq(state)
            states.append(state)
        return states

    def hops_back(own):
        states, state = [], own
        for last in range(nseq - 1, 0, -1):
            state = yield lax.ppermute(state, "seq", [(last, last - 1)])
            states.append(state)
            state = low_sum([own, passes * state.astype(f32)])
        return states

    def low_sum(terms):
        return total_of(terms).astype(bf16)

    def pair_step(terms, dim, bit, swap):
        arrived = yield swap(low_sum(take(terms, dim, 1 - bit)))
        return [*take(terms, dim, bit), arrived]

    def ring_step(pick):
        held = []
        for k in range(nseq - 1):
            block = lax.rem(si - 1 - k + 2 * nseq, nseq)
            arrived = yield over_seq(low_sum(pick(block) + held))
            held = [arrived]
        return pick(si) + held

    flat = tokens.reshape(stretch, width)
    seed = cotangent.reshape(stretch, width)
    branch0 = fence(seed.astype(bf16))
    branch1, branch2 = over_feat(branch0), over_x(branch0)

    ndocs = lengths.shape[1]
    doc_lengths = lax.dynamic_index_in_dim(lengths, fi * nrows + ri, 0, keepdims=False)
    starts = jnp.cumsum(doc_lengths) - doc_lengths
    offset = si * stretch

    def doc_of(places):
        return jnp.sum((starts[None, :] <= places[:, None]).astype(jnp.int32), axis=1)

    places = offset + jnp.arange(stretch, dtype=jnp.int32)
    docs = doc_of(places)
    away = jnp.arange(1, nseq, dtype=jnp.int32)
    before = doc_of(jnp.reshape(offset - 1, (1,)))
    final = doc_of(jnp.reshape(offset + stretch - 1, (1,)))
    causal = jnp.arange(stretch)[None, :] <= jnp.arange(stretch)[:, None]
    mask = ((docs[:, None] == docs[None, :]) & causal).astype(f32)
    from_before = jnp.broadcast_to((docs == before).astype(f32)[:, None], (stretch, 128))
    at_end = jnp.broadcast_to((docs == final).astype(f32)[:, None], (stretch, 128))
    earlier = (
        (doc_of(offset - 1 - (away - 1) * stretch) == before) & (away <= si)
    ).astype(f32)
    passes = (final == before).astype(f32)

    pick_a, pick_b, level = feature_tables()
    tables = [("state", pick_a), ("state", pick_b), ("all", level)]
    state_shape = (HEADS, STATE_ROWS, VHEAD)
    columns = ("all", (stretch, 128), f32)
    packed = (stretch, HEADS * FDIM)
    per_head = (stretch, width)

    root_one = lax.rsqrt(jnp.mean(flat * flat, axis=-1, keepdims=True) + EPS)
    low_one = (flat * root_one * gain_one).astype(bf16)
    low_one1 = over_feat(low_one)
    keys = mm(low_one, w_key).astype(bf16)
    values = mm(low_one, w_value).astype(bf16)
    (key_state,) = head_call(
        key_state_kernel,
        [*tables, ("all", keys), ("head", values), ("all", at_end)],
        [("state", state_shape, bf16)],
    )
    chain = Task(line, hops(fence(key_state)))
    queries = mm(fence(low_one), w_query).astype(bf16)
    numer, denom_here, feats = fence(
        *head_call(
            intra_kernel,
            [
                *tables,
                ("all", queries),
                ("all", keys),
                ("head", values),
                ("all", mask),
            ],
            [("head", per_head, f32), columns, ("state", (HEADS, stretch, PADF), bf16)],
        )
    )
    chain.step()

    def hidden_grad(g0, g1):
        return token_call(
            hidden_grad_kernel,
            which,
            stretch,
            [("pair", g0, g1), ("tall", w_down)],
            ["row"],
            width,
            slice_ff,
        )[0]

    def act(x0, x1, grad):
        return token_call(
            act_kernel,
            which,
            stretch,
            [("pair", x0, x1), ("row", grad), ("wide", w_gate), ("wide", w_up)],
            ["row"] * 3,
            width,
            slice_ff,
        )

    def low_grad(gg, gu, kind):
        return token_call(
            low_grad_kernel,
            which,
            stretch,
            [("row", gg), ("row", gu), ("wide", w_gate), ("wide", w_up)],
            [kind],
            width,
            slice_ff,
        )

    def layer(hid, kind):
        return token_call(
            layer_kernel,
            which,
            stretch,
            [("row", hid), ("tall", w_down)],
            [kind],
            width,
            slice_ff,
        )

    branch1, low_one1 = fence(branch1, low_one1)
    gh_near = fence(hidden_grad(branch0, branch1))
    chain.step()
    branch2 = fence(branch2)
    branch3 = over_feat(branch2)
    branch3 = fence(branch3)
    gh_far = fence(hidden_grad(branch2, branch3))
    states = chain.drain()

    mixed_low, denom, state_in = head_call(
        combine_kernel,
        [
            ("smem", earlier),
            ("state", feats),
            ("head", numer),
            ("all", denom_here),
            ("all", from_before),
            *(("state", s) for s in states),
        ],
        [("head", per_head, bf16), columns, ("state", state_shape, f32)],
    )
    mixed_low1 = over_feat(mixed_low)
    middle = flat + mm(mixed_low, w_out)
    root_two = lax.rsqrt(jnp.mean(middle * middle, axis=-1, keepdims=True) + EPS)
    low0 = fence((middle * root_two * gain_two).astype(bf16))
    low1, low2 = over_feat(low0), over_x(low0)

    mixed_low1, low1 = fence(mixed_low1, low1)
    hid_n, gg_n, gu_n = fence(*act(low0, low1, gh_near))
    glow0, glow1 = fence(*low_grad(gg_n, gu_n, "two"))
    glow1 = over_feat(glow1)
    low2 = fence(low2)
    low3 = over_feat(low2)
    low3, glow1 = fence(low3, glow1)
    hid_f, gg_f, gu_f = fence(*act(low2, low3, gh_far))

    lows = (low0, low1, low2, low3)
    branches = (branch0, branch1, branch2, branch3)
    group_rows = width // (2 * nseq)

    def wide_share(sent, kept):
        terms = [kept, (yield over_y(sent))]
        split = [t.reshape(2, nseq, 2, group_rows // 4, slice_ff) for t in terms]
        mine = yield from ring_step(lambda b: take(split, 1, b))
        mine = total_of(mine).astype(bf16)
        own = lax.dynamic_index_in_dim(mine, xb, 1, keepdims=False)
        other = yield over_x(lax.dynamic_index_in_dim(mine, 1 - xb, 1, keepdims=False))
        cols = jnp.where(
            xb == 0,
            jnp.concatenate([own, other], axis=-1),
            jnp.concatenate([other, own], axis=-1),
        )
        own = lax.dynamic_index_in_dim(cols, fi, 0, keepdims=False)
        other = yield over_feat(lax.dynamic_index_in_dim(cols, 1 - fi, 0, keepdims=False))
        return fence(
            jnp.where(
                fi == 0,
                jnp.concatenate([own, other], axis=-1),
                jnp.concatenate([other, own], axis=-1),
            ).astype(f32)
        )

    def down_share(sent, kept):
        rows = slice_ff // (2 * nseq)
        terms = [kept, (yield over_y(sent))]
        split = [t.reshape(nseq // 2, 2, rows, width) for t in terms]

        def pick(b):
            zero = jnp.int32(0)
            place = (b % (nseq // 2), b // (nseq // 2), zero, zero)
            return [
                lax.dynamic_slice(t, place, (1, 1, rows, width)).reshape(rows, width)
                for t in split
            ]

        mine = yield from ring_step(pick)
        mine = low_sum(mine)
        swaps = []
        for s in range(nseq):
            for r in range(nrows):
                x = s // (nseq // 2)
                if x != r % 2:
                    to = (r % 2) * (nseq // 2) + s % (nseq // 2)
                    swaps.append((s * nrows + r, to * nrows + (r ^ 1)))
        moved = yield lax.ppermute(mine, ("seq", "rows"), swaps)
        stays = (si // (nseq // 2)) == xb
        return fence(jnp.where(stays, mine, moved).astype(f32))

    down_parts = fence(
        *down_grad(ybit, fence(hid_n), hid_f, branches, slice_ff // (nseq // 2))
    )
    down = Task(line, down_share(*down_parts))
    glow2, *glow3 = fence(*low_grad(fence(gg_f), gu_f, "pair"))
    glow3 = [over_feat(g) for g in glow3]
    gate_parts = fence(*wide_grad(ybit, lows, fence(gg_n), gg_f, group_rows))
    glow2, *glow3 = fence(glow2, *glow3)
    far_glow = over_x(low_sum([glow2, jnp.concatenate(glow3)]))
    up_parts = fence(*wide_grad(ybit, lows, fence(gu_n), gu_f, group_rows))
    down.step()
    gate = Task(line, wide_share(*fence(*gate_parts)))
    lay0, *lay1 = fence(*layer(fence(hid_n), "pair"))
    lay1 = [over_feat(a) for a in lay1]

    grad_middle, grad_mixed_low, grad_mixed, gains_two, *copies = fence(
        *norm_back(glow0, glow1, fence(far_glow), middle, seed, gain_two, w_out)
    )
    copies = [over_feat(a) for a in copies]
    lay1 = list(fence(lay0, *lay1)[1:])

    query_state, gnum, gden = fence(
        *head_call(
            query_state_kernel,
            [
                ("state", feats),
                ("head", fence(grad_mixed)),
                ("head", mixed_low),
                ("all", denom),
                ("all", from_before),
            ],
            [("state", state_shape, bf16), ("head", per_head, bf16), columns],
        )
    )
    chain = Task(line, hops_back(query_state))
    down.step()
    lay2, *lay3 = fence(*layer(fence(hid_f), "pair"))
    lay3 = [over_feat(a) for a in lay3]

    part = width // (8 * nseq)

    def share(parts, along_x, order):
        sent, keep = parts
        terms = [keep, (yield (over_x if along_x else over_y)(sent))]
        dims = {"seq": 0, "y" if along_x else "x": 1}
        for name in order:
            dim = dims.pop(name)
            dims = {k: v - (v > dim) for k, v in dims.items()}
            if name == "seq":
                now = terms
                terms = yield from ring_step(lambda b: take(now, dim, b))
            else:
                bit, swap = {"x": (xb, over_x), "y": (yb, over_y)}[name]
                terms = yield from pair_step(terms, dim, bit, swap)
        return fence(total_of(terms))

    def back(heads, gq, gk, gv):
        return fence(
            *head_call(
                functools.partial(back_kernel, heads[0]),
                [
                    *tables,
                    ("all", queries),
                    ("all", keys),
                    ("head", values),
                    ("all", mask),
                    ("head", fence(gnum)),
                    ("all", gden),
                    ("state", state_in),
                    ("all", from_before),
                    ("all", gq),
                    ("all", gk),
                    ("any", gv),
                ],
                [("all", packed, f32), ("all", packed, f32), ("head", per_head, f32)],
                heads=heads,
                aliases={13: 2} if heads[0] else None,
            )
        )

    empty = jnp.zeros((8, 128), f32)
    chain.step()
    down.step()
    grads = back((0, HEADS // 2), empty, empty, empty)
    lay2, *lay3 = fence(lay2, *lay3)
    far_lay = over_x(low_sum([lay2, jnp.concatenate(lay3)]))
    chain.step()
    down.step()
    gate.step()
    up = Task(line, wide_share(*fence(*up_parts)))
    grad_mixed_low, *copies = fence(grad_mixed_low, *copies)
    out = []
    for place, order in enumerate((("y", "seq"), ("seq", "y"))):
        pieces = fence(
            *core_grad(
                bits,
                fence(mixed_low),
                mixed_low1,
                grad_mixed_low,
                copies,
                place,
                2,
                nseq,
                True,
            )
        )
        out.append(Task(line, share(pieces, True, order)))
    gq, gk_part, gv_part = back((HEADS // 2, HEADS), *grads)
    states = chain.drain()
    gate.step()
    down.step()
    grad_keys, grad_values_low = head_call(
        back_state_kernel,
        [
            ("smem", jnp.ones((nseq - 1,), f32)),
            *tables,
            ("all", keys),
            ("head", values),
            ("all", at_end),
            ("all", gk_part),
            ("head", gv_part),
            *(("state", s) for s in states),
        ],
        [("all", packed, bf16), ("head", per_head, bf16)],
        scratch=[pltpu.VMEM(packed, f32)],
    )
    grad_queries = gq.astype(bf16)
    half = (width + 2 * w_query.shape[1]) // 2
    grad_all = fence(
        grad_values_low[:, :half],
        jnp.concatenate([grad_values_low[:, half:], grad_queries, grad_keys], axis=-1),
    )
    grad_all1 = [over_feat(g) for g in grad_all]
    gate.step()
    layer_out = fence(middle + total_of([lay0, jnp.concatenate(lay1), fence(far_lay)]))
    inner = []
    for own, other, (along_x, order) in zip(
        grad_all, grad_all1, ((False, ("x", "seq")), (True, ("y", "seq")))
    ):
        pieces = fence(
            *core_grad(bits, low_one, low_one1, own, [fence(other)], 0, 1, nseq, along_x)
        )
        inner.append(Task(line, share(pieces, along_x, order)))
    grad_low_one = fence(
        mm(fence(grad_queries), w_query, NT)
        + mm(grad_keys, w_key, NT)
        + mm(grad_values_low, w_value, NT)
    )
    up.step()
    out[0].step()
    out[1].step()
    unit_one = flat * root_one
    grad_gain_one = jnp.sum(grad_low_one * unit_one, axis=0)
    scaled = grad_low_one * gain_one
    grad_tokens = grad_middle + root_one * (
        scaled - unit_one * jnp.mean(scaled * unit_one, axis=-1, keepdims=True)
    )
    grad_tokens, grad_gain_one = fence(grad_tokens, grad_gain_one)
    both = jnp.concatenate(
        [grad_gain_one.reshape(-1, part), gains_two[0].reshape(-1, part)], axis=-1
    )
    both = lax.all_to_all(both, ("feat", "seq", "rows"), 0, 0, tiled=True)
    tasks = [*inner, up, *out, gate, down]
    while not all(t.done for t in tasks):
        for t in tasks:
            t.step()
    gains = jnp.sum(fence(both), axis=0) + line.mark
    grad_out_w = jnp.concatenate([t.result for t in out], axis=-1)
    qk = w_query.shape[1]
    lower, upper = (t.result for t in inner)

    return (
        layer_out.reshape(rows_dev, stretch, width),
        grad_tokens.reshape(rows_dev, stretch, width),
        gains[:part],
        upper[:, width - half : width - half + qk],
        upper[:, width - half + qk :],
        jnp.concatenate([lower, upper[:, : width - half]], axis=-1),
        grad_out_w,
        gains[part:],
        gate.result,
        up.result,
        down.result,
    )


def solution(mesh):
    split = P(("feat", "rows"), "seq", None)
    vector = P(("feat", "seq", "rows"))
    matrix = P(("feat", "seq", "rows"), None)
    in_specs = (split, *(P() for _ in range(10)), split)
    out_specs = (
        split,
        split,
        vector,
        matrix,
        matrix,
        matrix,
        matrix,
        vector,
        matrix,
        matrix,
        matrix,
    )
    return jax.shard_map(shards, mesh=mesh, in_specs=in_specs, out_specs=out_specs, check_vma=False)
```

```python
import functools

import jax
import jax.numpy as jnp
import ml_dtypes
import numpy as np
from jax import lax
from jax.experimental import pallas as pl
from jax.experimental.pallas import tpu as pltpu
from jax.sharding import PartitionSpec as P

HEADS = 16
FDIM = 16
VHEAD = 128
EPS = 1e-06

bf16 = jnp.bfloat16
f32 = jnp.float32

PAIRS = [(a, b) for a in range(FDIM + 1) for b in range(a, FDIM + 1)]
NPAIR = len(PAIRS)
PADF = 256
STATE_ROWS = 160
VMEM_MIB = 30
bf16 = jnp.bfloat16
f32 = jnp.float32

PAIRS = [(a, b) for a in range(FDIM + 1) for b in range(a, FDIM + 1)]
NPAIR = len(PAIRS)
PADF = 256
STATE_ROWS = 160
VMEM_MIB = 30
SCALE = 20

NN = (((1,), (0,)), ((), ()))
NT = (((1,), (1,)), ((), ()))
TN = (((0,), (0,)), ((), ()))


def mm(a, b, dims=NN):
    return lax.dot_general(a, b, dims, preferred_element_type=f32)


def feature_tables():
    level = np.zeros((8, PADF), np.float32)
    for f, (a, b) in enumerate(PAIRS):
        level[0, f] = float(a == FDIM)
        level[1, f] = float(b == FDIM)
        if a == FDIM:
            level[2, f] = 1.0
        elif b == FDIM:
            level[2, f] = FDIM**-0.5
        elif a == b:
            level[2, f] = 1.0 / (2 * FDIM)
        else:
            level[2, f] = 1.0 / FDIM
    pick = np.zeros((2, HEADS, HEADS * FDIM, PADF), np.float32)
    for head in range(HEADS):
        for f, pair in enumerate(PAIRS):
            for k, entry in enumerate(pair):
                if entry < FDIM:
                    pick[k, head, head * FDIM + entry, f] = 1.0
    pick = pick.astype(ml_dtypes.bfloat16)
    return jnp.asarray(pick[0]), jnp.asarray(pick[1]), jnp.asarray(level)


FREE = pl.CostEstimate(flops=0, bytes_accessed=0, transcendentals=0)


def params(mib):
    return pltpu.CompilerParams(vmem_limit_bytes=mib << 20)


def factors(packed, pick_a, pick_b, level):
    return mm(packed, pick_a[0]) + level[0:1, :], mm(packed, pick_b[0]) + level[1:2, :]


def wide(value, times):
    return jnp.concatenate([value] * times, axis=1)


def parts(value):
    high = value.astype(bf16)
    return high, (value - high.astype(f32)).astype(bf16)


def own_lanes(head, packed):
    lane = lax.broadcasted_iota(jnp.int32, packed.shape, 1)
    return jnp.where(lane // FDIM == head, packed, jnp.zeros_like(packed))


def pack_state(state, sums):
    block = state[:STATE_ROWS]
    high = sums.astype(bf16).astype(f32)
    low = sums - high
    row = lax.broadcasted_iota(jnp.int32, block.shape, 0)
    for k, part in enumerate((high[:, :128], high[:, 128:], low[:, :128], low[:, 128:])):
        block = jnp.where(row == NPAIR + k, part, block)
    return block.astype(bf16)


def unpack_state(block):
    row = lax.broadcasted_iota(jnp.int32, block.shape, 0)

    def line(k):
        return jnp.sum(jnp.where(row == NPAIR + k, block, 0.0), axis=0, keepdims=True)

    sums = jnp.concatenate([line(0) + line(2), line(1) + line(3)], axis=1)
    state = jnp.where(row < NPAIR, block, 0.0).astype(bf16)
    pad = jnp.zeros((PADF - STATE_ROWS, VHEAD), bf16)
    return jnp.concatenate([state, pad], axis=0), sums


def sum_against(feats, sums):
    return sum(mm(feats, p, NT) for p in parts(jnp.broadcast_to(sums, (128, PADF))))


def column(ref, head):
    row = lax.broadcasted_iota(jnp.int32, (128, 128), 0)
    pick = jnp.where(row == head, 1.0, 0.0).astype(bf16)
    return sum(mm(p, pick) for p in parts(ref[...]))


def row_sum(value):
    ones = jnp.ones((128, 128), bf16)
    return sum(mm(p, ones) for p in parts(value))


def set_column(ref, head, value):
    lane = lax.broadcasted_iota(jnp.int32, ref.shape, 1)

    @pl.when(head == 0)
    def _():
        ref[...] = jnp.zeros_like(ref)

    ref[...] = jnp.where(lane == head, value, ref[...])


def key_state_kernel(head, pick_a, pick_b, level, k_ref, v_ref, end_ref, out_ref):
    one, two = factors(k_ref[...], pick_a, pick_b, level)
    feats = (one * two * wide(end_ref[...], 2)).astype(bf16)
    state = mm(feats, v_ref[...], TN)
    sums = jnp.sum(feats.astype(f32), axis=0, keepdims=True)
    out_ref[0] = pack_state(state, sums)


def intra_kernel(head, pick_a, pick_b, level, q_ref, k_ref, v_ref, mask_ref, num_ref, den_ref, feat_ref):
    queries = q_ref[...]
    scores = mm(own_lanes(head, queries), k_ref[...], NT)
    lin = scores * 0.25 + 1.0
    weights = ((lin * lin * 0.5 + 0.5) * mask_ref[...]).astype(bf16)
    values = v_ref[...]
    both = mm(weights, jnp.concatenate([values, jnp.ones_like(values)], axis=1))
    num_ref[...] = both[:, :VHEAD]
    set_column(den_ref, head, both[:, VHEAD:])
    one, two = factors(queries, pick_a, pick_b, level)
    feat_ref[0] = (one * two * level[2:3, :]).astype(bf16)


def kept_state(kept_ref, state_refs):
    block = jnp.zeros(state_refs[0].shape[1:], f32)
    for k, ref in enumerate(state_refs):
        block = block + kept_ref[k] * ref[0].astype(f32)
    return block


def combine_kernel(head, kept_ref, feat_ref, num_ref, den_ref, from_ref, *refs):
    *state_refs, mixed_ref, total_ref, block_ref = refs
    feats = feat_ref[0]
    block = kept_state(kept_ref, state_refs)
    block_ref[0] = block
    state, sums = unpack_state(block)
    reach = from_ref[...]
    den = column(den_ref, head) + reach * sum_against(feats, sums)
    mixed_ref[...] = ((num_ref[...] + reach * mm(feats, state)) * (1.0 / den)).astype(bf16)
    set_column(total_ref, head, den)


def query_state_kernel(
    head, feat_ref, grad_ref, mixed_ref, den_ref, from_ref, out_ref, gnum_ref, gden_ref
):
    feats = feat_ref[0]
    gnum = (grad_ref[...] * (1.0 / column(den_ref, head))).astype(bf16)
    far = gnum.astype(f32)
    gden = -row_sum(far * mixed_ref[...].astype(f32))
    reach = from_ref[...]
    state = mm(feats, (far * reach).astype(bf16), TN)
    sums = jnp.sum(feats.astype(f32) * wide(gden * reach, 2), axis=0, keepdims=True)
    out_ref[0] = pack_state(state, sums)
    gnum_ref[...] = gnum
    set_column(gden_ref, head, gden)


def back_kernel(
    first,
    head,
    pick_a,
    pick_b,
    level,
    q_ref,
    k_ref,
    v_ref,
    mask_ref,
    gnum_ref,
    gden_ref,
    state_ref,
    from_ref,
    gq_in,
    gk_in,
    gv_in,
    gq_ref,
    gk_ref,
    gv_ref,
):
    queries, keys, values = q_ref[...], k_ref[...], v_ref[...]
    gnum = gnum_ref[...]
    gden = column(gden_ref, head)
    q_own, k_own = own_lanes(head, queries), own_lanes(head, keys)
    scores = mm(q_own, keys, NT)
    lin = scores * 0.25 + 1.0
    mask = mask_ref[...]
    weights = ((lin * lin * 0.5 + 0.5) * mask).astype(bf16)
    spread = wide(gden, keys.shape[0] // 128)
    slopes = ((mm(gnum, values, NT) + spread) * (mask * lin * 0.25)).astype(bf16)
    gv_ref[...] = mm(weights, gnum, TN)
    grad_q = mm(slopes, k_own)
    grad_k = mm(slopes, q_own, TN)

    one, two = factors(queries, pick_a, pick_b, level)
    state, sums = unpack_state(state_ref[0])
    reach = from_ref[...]
    gfeat = (mm(gnum, state, NT) + wide(gden, 2) * sums) * wide(reach, 2) * level[2:3, :]
    grad_q += mm((gfeat * two).astype(bf16), pick_a[0], NT)
    grad_q += mm((gfeat * one).astype(bf16), pick_b[0], NT)

    @pl.when(head == first)
    def _():
        if first == 0:
            gq_ref[...] = jnp.zeros_like(gq_ref)
            gk_ref[...] = jnp.zeros_like(gk_ref)
        else:
            gq_ref[...] = gq_in[...]
            gk_ref[...] = gk_in[...]

    gq_ref[...] += grad_q
    gk_ref[...] += grad_k


def back_state_kernel(
    head, kept_ref, pick_a, pick_b, level, k_ref, v_ref, end_ref, gk_in, gv_in, *refs
):
    *state_refs, gk_ref, gv_ref, gk_sum = refs
    values = v_ref[...]
    one, two = factors(k_ref[...], pick_a, pick_b, level)
    state, sums = unpack_state(kept_state(kept_ref, state_refs))
    reach = wide(end_ref[...], 2)
    feats = (one * two * reach).astype(bf16)
    gv_ref[...] = (gv_in[...] + mm(feats, state)).astype(bf16)
    gfeat = (mm(values, state, NT) + sums) * reach
    grad_k = mm((gfeat * two).astype(bf16), pick_a[0], NT)
    grad_k += mm((gfeat * one).astype(bf16), pick_b[0], NT)

    @pl.when(head == 0)
    def _():
        gk_sum[...] = gk_in[...]

    gk_sum[...] += grad_k

    @pl.when(head == HEADS - 1)
    def _():
        gk_ref[...] = gk_sum[...].astype(bf16)


def head_call(kernel, ins, outs, heads=(0, HEADS), scratch=(), aliases=None):
    first, last = heads

    def spec(kind, shape):
        if kind == "all":
            return pl.BlockSpec(shape, lambda h: (0,) * len(shape))
        if kind == "head":
            return pl.BlockSpec((shape[0], VHEAD), lambda h: (0, h + first))
        if kind == "state":
            return pl.BlockSpec((1, *shape[1:]), lambda h: (h + first, 0, 0))
        if kind == "smem":
            return pl.BlockSpec(memory_space=pltpu.SMEM)
        return pl.BlockSpec(memory_space=pl.ANY)

    def body(*refs):
        kernel(pl.program_id(0) + first, *refs)

    return pl.pallas_call(
        body,
        grid=(last - first,),
        in_specs=[spec(kind, a.shape) for kind, a in ins],
        out_specs=[spec(kind, shape) for kind, shape, _ in outs],
        out_shape=[sds(shape, dtype) for _, shape, dtype in outs],
        scratch_shapes=list(scratch),
        input_output_aliases=aliases or {},
        compiler_params=params(20),
        cost_estimate=FREE,
    )(*(a for _, a in ins))


def sds(shape, dtype):
    return jax.ShapeDtypeStruct(shape, dtype)


def hidden_grad_kernel(half, which_ref, g0, g1, wd, out):
    branch = jnp.where(pl.program_id(0) < half, g0[...], g1[...])
    out[...] = mm(branch, wd[...], NT).astype(bf16)


def act_kernel(half, which_ref, x0, x1, grad_ref, wg, wu, hid, gg, gu):
    tokens = jnp.where(pl.program_id(0) < half, x0[...], x1[...])
    gate = mm(tokens, wg[...])
    up = mm(tokens, wu[...])
    grad = grad_ref[...].astype(f32)
    sig = 1.0 / (1.0 + jnp.exp(-gate))
    silu = gate * sig
    hid[...] = (silu * up).astype(bf16)
    gg[...] = (grad * up * (sig * (1.0 + gate * (1.0 - sig)))).astype(bf16)
    gu[...] = (grad * silu).astype(bf16)


def put(half, value, low, pieces):
    step = pl.program_id(0)

    @pl.when(step < half)
    def _():
        low[...] = value

    for k, piece in enumerate(pieces):
        here = step == half + k if len(pieces) > 1 else step >= half

        @pl.when(here)
        def _(piece=piece):
            piece[...] = value


def low_grad_kernel(half, which_ref, gg, gu, wg, wu, low, *pieces):
    value = (mm(gg[...], wg[...], NT) + mm(gu[...], wu[...], NT)).astype(bf16)
    put(half, value, low, pieces)


def layer_kernel(half, which_ref, hid, wd, low, *pieces):
    put(half, mm(hid[...], wd[...]).astype(bf16), low, pieces)


def token_call(kernel, which, count, ins, outs, width, slice_ff):
    tile = min(256, count)
    half = count // tile
    once = pl.Buffered(1)
    low = pl.BlockSpec((tile, width), lambda i, w: (jnp.minimum(i, half - 1), 0))
    high = pl.BlockSpec((tile, width), lambda i, w: (jnp.maximum(i - half, 0), 0))
    row = pl.BlockSpec((tile, slice_ff), lambda i, w: (i, 0))
    specs, operands = [], []
    for kind, *arrays in ins:
        operands += arrays
        specs += {
            "pair": [low, high],
            "row": [row],
            "wide": [pl.BlockSpec((width, slice_ff), lambda i, w: (0, w[0]), pipeline_mode=once)],
            "tall": [pl.BlockSpec((slice_ff, width), lambda i, w: (w[0], 0), pipeline_mode=once)],
        }[kind]
    out_specs, out_shapes = [], []
    for kind in outs:
        if kind == "row":
            out_specs.append(row)
            out_shapes.append(sds((2 * count, slice_ff), bf16))
        elif kind == "two":
            out_specs += [low, high]
            out_shapes += [sds((count, width), bf16)] * 2
        else:
            piece = pl.BlockSpec((tile, width), lambda i, w: (0, 0))
            out_specs += [low] + [piece] * half
            out_shapes += [sds((count, width), bf16)] + [sds((tile, width), bf16)] * half
    return pl.pallas_call(
        functools.partial(kernel, half),
        grid_spec=pltpu.PrefetchScalarGridSpec(
            num_scalar_prefetch=1,
            grid=(2 * half,),
            in_specs=specs,
            out_specs=out_specs,
        ),
        out_shape=out_shapes,
        compiler_params=params(VMEM_MIB),
        cost_estimate=FREE,
    )(which, *operands)


def split_rows(total, high, send, keep):
    groups = send.shape[0]
    rows = total.shape[0] // groups
    for g in range(groups):
        a = total[g * rows : g * rows + rows // 2]
        b = total[g * rows + rows // 2 : (g + 1) * rows]
        send[g] = jnp.where(high, a, b).astype(bf16)
        keep[g] = jnp.where(high, b, a).astype(bf16)


def wide_grad_kernel(ybit_ref, l0, l1, l2, l3, near, far, send, keep):
    count = l0.shape[0]
    total = mm(l0[...], near[:count, :], TN)
    total += mm(l1[...], near[count:, :], TN)
    total += mm(l2[...], far[:count, :], TN)
    total += mm(l3[...], far[count:, :], TN)
    split_rows(total, ybit_ref[0] == 1, send, keep)


def wide_grad(ybit, lows, near, far, group_rows):
    count, width = lows[0].shape
    cols = near.shape[1]
    tile = min(256, width)
    groups = tile // group_rows
    lane = pl.BlockSpec((count, tile), lambda i, w: (0, i))
    held = pl.BlockSpec((2 * count, cols), lambda i, w: (0, 0), pipeline_mode=pl.Buffered(1))
    out = pl.BlockSpec((groups, group_rows // 2, cols), lambda i, w: (i, 0, 0))
    shape = sds((width // group_rows, group_rows // 2, cols), bf16)
    return pl.pallas_call(
        wide_grad_kernel,
        grid_spec=pltpu.PrefetchScalarGridSpec(
            num_scalar_prefetch=1,
            grid=(width // tile,),
            in_specs=[lane, lane, lane, lane, held, held],
            out_specs=[out, out],
        ),
        out_shape=[shape, shape],
        compiler_params=params(VMEM_MIB),
        cost_estimate=FREE,
    )(ybit, *lows, near, far)


def down_grad_kernel(ybit_ref, near, far, g0, g1, g2, g3, send, keep):
    count = g0.shape[0]
    total = mm(near[:count, :], g0[...], TN)
    total += mm(near[count:, :], g1[...], TN)
    total += mm(far[:count, :], g2[...], TN)
    total += mm(far[count:, :], g3[...], TN)
    split_rows(total, ybit_ref[0] == 1, send, keep)


def down_grad(ybit, near, far, grads, group_rows):
    count, width = grads[0].shape
    rows = near.shape[1]
    tile = min(256, width)
    lane = pl.BlockSpec((count, tile), lambda i, w: (0, i))
    held = pl.BlockSpec((2 * count, rows), lambda i, w: (0, 0), pipeline_mode=pl.Buffered(1))
    out = pl.BlockSpec((rows // group_rows, group_rows // 2, tile), lambda i, w: (0, 0, i))
    shape = sds((rows // group_rows, group_rows // 2, width), bf16)
    return pl.pallas_call(
        down_grad_kernel,
        grid_spec=pltpu.PrefetchScalarGridSpec(
            num_scalar_prefetch=1,
            grid=(width // tile,),
            in_specs=[held, held, lane, lane, lane, lane],
            out_specs=[out, out],
        ),
        out_shape=[shape, shape],
        compiler_params=params(VMEM_MIB),
        cost_estimate=FREE,
    )(ybit, near, far, *grads)


def norm_back_kernel(low, near, far, middle, seed, gain, w, grad_ref, low_ref, mixed_ref, gain_ref, *copies):
    grad = low[...].astype(f32) + near[...].astype(f32) + far[...].astype(f32)
    value = middle[...]
    root = lax.rsqrt(jnp.mean(value * value, axis=-1, keepdims=True) + EPS)
    unit = value * root

    @pl.when(pl.program_id(0) == 0)
    def _():
        gain_ref[...] = jnp.zeros_like(gain_ref)

    gain_ref[...] += jnp.broadcast_to(jnp.sum(grad * unit, axis=0, keepdims=True), gain_ref.shape)
    scaled = grad * gain[...]
    total = seed[...] + root * (scaled - unit * jnp.mean(scaled * unit, axis=-1, keepdims=True))
    grad_ref[...] = total
    narrow = total.astype(bf16)
    low_ref[...] = narrow
    for k, copy in enumerate(copies):

        @pl.when(pl.program_id(0) == k)
        def _(copy=copy):
            copy[...] = narrow

    mixed_ref[...] = mm(narrow, w[...], NT).astype(bf16)


def norm_back(low, near, far, middle, seed, gain, w):
    count, width = middle.shape
    tile = min(256, count)
    halves = count // tile
    row = pl.BlockSpec((tile, width), lambda i: (i, 0))

    def held(shape):
        return pl.BlockSpec(shape, lambda i: (0, 0), pipeline_mode=pl.Buffered(1))

    return pl.pallas_call(
        norm_back_kernel,
        grid=(count // tile,),
        in_specs=[row] * 5 + [held((1, width)), held(w.shape)],
        out_specs=[row] * 3
        + [pl.BlockSpec((8, width), lambda i: (0, 0))]
        + [
            pl.BlockSpec((tile, width), lambda i: (0, 0)) for _ in range(halves)
        ],
        out_shape=[
            sds((count, width), f32),
            sds((count, width), bf16),
            sds((count, width), bf16),
            sds((8, width), f32),
            *[sds((tile, width), bf16)] * halves,
        ],
        compiler_params=params(50),
        cost_estimate=FREE,
    )(low, near, far, middle, seed, gain.reshape(1, width), w)


def core_grad_kernel(along_x, bits_ref, r0, r1, c0, *refs):
    *others, send, keep = refs
    total = mm(r0[...], c0[...], TN)
    first = 0
    for c1 in others:
        count = c1.shape[0]
        total += mm(r1[first : first + count, :], c1[...], TN)
        first += count
    groups, _, rows, _ = send.shape
    high = bits_ref[1 if along_x else 2] == 1
    for g in range(groups):

        def block(y, x):
            first = (4 * g + 2 * y + x) * rows
            return total[first : first + rows]

        for k in range(2):
            a, b = (block(k, 0), block(k, 1)) if along_x else (block(0, k), block(1, k))
            send[g, k] = jnp.where(high, a, b).astype(bf16)
            keep[g, k] = jnp.where(high, b, a).astype(bf16)


def core_grad(bits, r0, r1, c0, others, place, parts, nseq, along_x):
    count, width = r0.shape
    cols = c0.shape[1] // parts
    tile = min(256, width // 2)
    steps = width // 2 // tile
    rows = width // (8 * nseq)
    groups = tile // (4 * rows)
    lane = pl.BlockSpec((count, tile), lambda i, w: (0, w[0] * steps + i))

    def held(a):
        return pl.BlockSpec(
            (a.shape[0], cols), lambda i, w: (0, place), pipeline_mode=pl.Buffered(1)
        )

    out = pl.BlockSpec((groups, 2, rows, cols), lambda i, w: (i, 0, 0, 0))
    return pl.pallas_call(
        functools.partial(core_grad_kernel, along_x),
        grid_spec=pltpu.PrefetchScalarGridSpec(
            num_scalar_prefetch=1,
            grid=(steps,),
            in_specs=[lane, lane, held(c0), *(held(c) for c in others)],
            out_specs=[out, out],
        ),
        out_shape=[sds((nseq, 2, rows, cols), bf16)] * 2,
        compiler_params=params(VMEM_MIB),
        cost_estimate=FREE,
    )(bits, r0, r1, c0, *others)


def total_of(terms):
    total = terms[0].astype(f32)
    for term in terms[1:]:
        total = total + term.astype(f32)
    return total


def take(terms, dim, place):
    return [lax.dynamic_index_in_dim(t, place, dim, keepdims=False) for t in terms]


class Line:
    def __init__(self, mark):
        self.mark = mark

    def fence(self, *values):
        *values, self.mark = lax.optimization_barrier((*values, self.mark))
        return values[0] if len(values) == 1 else tuple(values)


class Task:
    def __init__(self, line, chain):
        self.line, self.chain, self.done = line, chain, False
        self.result = None
        self.waiting = next(chain)

    def step(self, count=1):
        for _ in range(count):
            if self.done:
                return
            try:
                self.waiting = self.chain.send(self.line.fence(self.waiting))
            except StopIteration as end:
                self.done, self.result = True, end.value

    def drain(self):
        while not self.done:
            self.step()
        return self.result


def shards(
    tokens,
    lengths,
    gain_one,
    w_query,
    w_key,
    w_value,
    w_out,
    gain_two,
    w_gate,
    w_up,
    w_down,
    cotangent,
):
    rows_dev, stretch, width = tokens.shape
    nfeat, nseq, nrows = (lax.axis_size(a) for a in ("feat", "seq", "rows"))
    assert rows_dev == 1 and nfeat == 2 and nrows == 4 and nseq % 2 == 0
    ff = w_gate.shape[1]
    fi, si, ri = (lax.axis_index(a) for a in ("feat", "seq", "rows"))
    xb, yb = ri % 2, ri // 2
    slice_ff = ff // 4
    which = jnp.reshape(2 * fi + xb, (1,)).astype(jnp.int32)
    ybit = jnp.reshape(yb, (1,)).astype(jnp.int32)
    bits = jnp.stack([fi, xb, yb]).astype(jnp.int32)

    line = Line((lengths[0, :1] < 0).astype(f32))
    fence = line.fence

    def over_feat(a):
        return lax.ppermute(a, "feat", [(0, 1), (1, 0)])

    def over_x(a):
        return lax.ppermute(a, "rows", [(r, r ^ 1) for r in range(nrows)])

    def over_y(a):
        return lax.ppermute(a, "rows", [(r, r ^ 2) for r in range(nrows)])

    def over_seq(a, shift=1):
        return lax.ppermute(a, "seq", [(s, (s + shift) % nseq) for s in range(nseq)])

    depth = nseq.bit_length() - 1
    assert nseq == 1 << depth

    def over_bit(k, a):
        return lax.ppermute(a, "seq", [(s, s ^ (1 << k)) for s in range(nseq)])

    def hops(state):
        states = []
        for _ in range(nseq - 1):
            state = yield over_seq(state)
            states.append(state)
        return states

    def hops_back(own):
        states, state = [], own
        for last in range(nseq - 1, 0, -1):
            state = yield lax.ppermute(state, "seq", [(last, last - 1)])
            states.append(state)
            state = low_sum([own, passes * state.astype(f32)])
        return states

    def low_sum(terms):
        return total_of(terms).astype(bf16)

    def pair_step(terms, dim, bit, swap):
        arrived = yield swap(low_sum(take(terms, dim, 1 - bit)))
        return [*take(terms, dim, bit), arrived]

    def ring_step(pick):
        held = []
        for k in range(nseq - 1):
            block = lax.rem(si - 1 - k + 2 * nseq, nseq)
            arrived = yield over_seq(low_sum(pick(block) + held))
            held = [arrived]
        return pick(si) + held

    flat = tokens.reshape(stretch, width)
    seed = cotangent.reshape(stretch, width)
    branch0 = fence(seed.astype(bf16))
    branch1, branch2 = over_feat(branch0), over_x(branch0)

    ndocs = lengths.shape[1]
    doc_lengths = lax.dynamic_index_in_dim(lengths, fi * nrows + ri, 0, keepdims=False)
    starts = jnp.cumsum(doc_lengths) - doc_lengths
    offset = si * stretch

    def doc_of(places):
        return jnp.sum((starts[None, :] <= places[:, None]).astype(jnp.int32), axis=1)

    places = offset + jnp.arange(stretch, dtype=jnp.int32)
    docs = doc_of(places)
    away = jnp.arange(1, nseq, dtype=jnp.int32)
    before = doc_of(jnp.reshape(offset - 1, (1,)))
    final = doc_of(jnp.reshape(offset + stretch - 1, (1,)))
    causal = jnp.arange(stretch)[None, :] <= jnp.arange(stretch)[:, None]
    mask = ((docs[:, None] == docs[None, :]) & causal).astype(f32)
    from_before = jnp.broadcast_to((docs == before).astype(f32)[:, None], (stretch, 128))
    at_end = jnp.broadcast_to((docs == final).astype(f32)[:, None], (stretch, 128))
    earlier = (
        (doc_of(offset - 1 - (away - 1) * stretch) == before) & (away <= si)
    ).astype(f32)
    passes = (final == before).astype(f32)

    pick_a, pick_b, level = feature_tables()
    tables = [("state", pick_a), ("state", pick_b), ("all", level)]
    state_shape = (HEADS, STATE_ROWS, VHEAD)
    columns = ("all", (stretch, 128), f32)
    packed = (stretch, HEADS * FDIM)
    per_head = (stretch, width)

    root_one = lax.rsqrt(jnp.mean(flat * flat, axis=-1, keepdims=True) + EPS)
    low_one = (flat * root_one * gain_one).astype(bf16)
    low_one1 = over_feat(low_one)
    keys = mm(low_one, w_key).astype(bf16)
    values = mm(low_one, w_value).astype(bf16)
    (key_state,) = head_call(
        key_state_kernel,
        [*tables, ("all", keys), ("head", values), ("all", at_end)],
        [("state", state_shape, bf16)],
    )
    chain = Task(line, hops(fence(key_state)))
    queries = mm(fence(low_one), w_query).astype(bf16)
    numer, denom_here, feats = fence(
        *head_call(
            intra_kernel,
            [
                *tables,
                ("all", queries),
                ("all", keys),
                ("head", values),
                ("all", mask),
            ],
            [("head", per_head, f32), columns, ("state", (HEADS, stretch, PADF), bf16)],
        )
    )
    chain.step()

    def hidden_grad(g0, g1):
        return token_call(
            hidden_grad_kernel,
            which,
            stretch,
            [("pair", g0, g1), ("tall", w_down)],
            ["row"],
            width,
            slice_ff,
        )[0]

    def act(x0, x1, grad):
        return token_call(
            act_kernel,
            which,
            stretch,
            [("pair", x0, x1), ("row", grad), ("wide", w_gate), ("wide", w_up)],
            ["row"] * 3,
            width,
            slice_ff,
        )

    def low_grad(gg, gu, kind):
        return token_call(
            low_grad_kernel,
            which,
            stretch,
            [("row", gg), ("row", gu), ("wide", w_gate), ("wide", w_up)],
            [kind],
            width,
            slice_ff,
        )

    def layer(hid, kind):
        return token_call(
            layer_kernel,
            which,
            stretch,
            [("row", hid), ("tall", w_down)],
            [kind],
            width,
            slice_ff,
        )

    branch1, low_one1 = fence(branch1, low_one1)
    gh_near = fence(hidden_grad(branch0, branch1))
    chain.step()
    branch2 = fence(branch2)
    branch3 = over_feat(branch2)
    branch3 = fence(branch3)
    gh_far = fence(hidden_grad(branch2, branch3))
    states = chain.drain()

    mixed_low, denom, state_in = head_call(
        combine_kernel,
        [
            ("smem", earlier),
            ("state", feats),
            ("head", numer),
            ("all", denom_here),
            ("all", from_before),
            *(("state", s) for s in states),
        ],
        [("head", per_head, bf16), columns, ("state", state_shape, f32)],
    )
    mixed_low1 = over_feat(mixed_low)
    middle = flat + mm(mixed_low, w_out)
    root_two = lax.rsqrt(jnp.mean(middle * middle, axis=-1, keepdims=True) + EPS)
    low0 = fence((middle * root_two * gain_two).astype(bf16))
    low1, low2 = over_feat(low0), over_x(low0)

    mixed_low1, low1 = fence(mixed_low1, low1)
    hid_n, gg_n, gu_n = fence(*act(low0, low1, gh_near))
    glow0, glow1 = fence(*low_grad(gg_n, gu_n, "two"))
    glow1 = over_feat(glow1)
    low2 = fence(low2)
    low3 = over_feat(low2)
    low3, glow1 = fence(low3, glow1)
    hid_f, gg_f, gu_f = fence(*act(low2, low3, gh_far))

    lows = (low0, low1, low2, low3)
    branches = (branch0, branch1, branch2, branch3)
    group_rows = width // (2 * nseq)

    def wide_share(sent, kept):
        terms = [kept, (yield over_y(sent))]
        split = [t.reshape(2, nseq, 2, group_rows // 4, slice_ff) for t in terms]
        mine = yield from ring_step(lambda b: take(split, 1, b))
        mine = total_of(mine).astype(bf16)
        own = lax.dynamic_index_in_dim(mine, xb, 1, keepdims=False)
        other = yield over_x(lax.dynamic_index_in_dim(mine, 1 - xb, 1, keepdims=False))
        cols = jnp.where(
            xb == 0,
            jnp.concatenate([own, other], axis=-1),
            jnp.concatenate([other, own], axis=-1),
        )
        own = lax.dynamic_index_in_dim(cols, fi, 0, keepdims=False)
        other = yield over_feat(lax.dynamic_index_in_dim(cols, 1 - fi, 0, keepdims=False))
        return fence(
            jnp.where(
                fi == 0,
                jnp.concatenate([own, other], axis=-1),
                jnp.concatenate([other, own], axis=-1),
            ).astype(f32)
        )

    def down_share(sent, kept):
        rows = slice_ff // (2 * nseq)
        terms = [kept, (yield over_y(sent))]
        split = [t.reshape(nseq // 2, 2, rows, width) for t in terms]

        def pick(b):
            zero = jnp.int32(0)
            place = (b % (nseq // 2), b // (nseq // 2), zero, zero)
            return [
                lax.dynamic_slice(t, place, (1, 1, rows, width)).reshape(rows, width)
                for t in split
            ]

        mine = yield from ring_step(pick)
        mine = low_sum(mine)
        swaps = []
        for s in range(nseq):
            for r in range(nrows):
                x = s // (nseq // 2)
                if x != r % 2:
                    to = (r % 2) * (nseq // 2) + s % (nseq // 2)
                    swaps.append((s * nrows + r, to * nrows + (r ^ 1)))
        moved = yield lax.ppermute(mine, ("seq", "rows"), swaps)
        stays = (si // (nseq // 2)) == xb
        return fence(jnp.where(stays, mine, moved).astype(f32))

    down_parts = fence(
        *down_grad(ybit, fence(hid_n), hid_f, branches, slice_ff // (nseq // 2))
    )
    down = Task(line, down_share(*down_parts))
    glow2, *glow3 = fence(*low_grad(fence(gg_f), gu_f, "pair"))
    glow3 = [over_feat(g) for g in glow3]
    gate_parts = fence(*wide_grad(ybit, lows, fence(gg_n), gg_f, group_rows))
    glow2, *glow3 = fence(glow2, *glow3)
    far_glow = over_x(low_sum([glow2, jnp.concatenate(glow3)]))
    up_parts = fence(*wide_grad(ybit, lows, fence(gu_n), gu_f, group_rows))
    down.step()
    gate = Task(line, wide_share(*fence(*gate_parts)))
    lay0, *lay1 = fence(*layer(fence(hid_n), "pair"))
    lay1 = [over_feat(a) for a in lay1]

    grad_middle, grad_mixed_low, grad_mixed, gains_two, *copies = fence(
        *norm_back(glow0, glow1, fence(far_glow), middle, seed, gain_two, w_out)
    )
    copies = [over_feat(a) for a in copies]
    lay1 = list(fence(lay0, *lay1)[1:])

    query_state, gnum, gden = fence(
        *head_call(
            query_state_kernel,
            [
                ("state", feats),
                ("head", fence(grad_mixed)),
                ("head", mixed_low),
                ("all", denom),
                ("all", from_before),
            ],
            [("state", state_shape, bf16), ("head", per_head, bf16), columns],
        )
    )
    chain = Task(line, hops_back(query_state))
    down.step()
    lay2, *lay3 = fence(*layer(fence(hid_f), "pair"))
    lay3 = [over_feat(a) for a in lay3]

    part = width // (8 * nseq)

    def share(parts, along_x, order):
        sent, keep = parts
        terms = [keep, (yield (over_x if along_x else over_y)(sent))]
        dims = {"seq": 0, "y" if along_x else "x": 1}
        for name in order:
            dim = dims.pop(name)
            dims = {k: v - (v > dim) for k, v in dims.items()}
            if name == "seq":
                terms = [t.reshape(*t.shape[:dim], *[2] * depth, *t.shape[dim + 1 :]) for t in terms]
                for k in range(depth):
                    terms = yield from pair_step(
                        terms, dim + depth - 1 - k, (si >> k) & 1, functools.partial(over_bit, k)
                    )
            else:
                bit, swap = {"x": (xb, over_x), "y": (yb, over_y)}[name]
                terms = yield from pair_step(terms, dim, bit, swap)
        return fence(total_of(terms))

    def back(heads, gq, gk, gv):
        return fence(
            *head_call(
                functools.partial(back_kernel, heads[0]),
                [
                    *tables,
                    ("all", queries),
                    ("all", keys),
                    ("head", values),
                    ("all", mask),
                    ("head", fence(gnum)),
                    ("all", gden),
                    ("state", state_in),
                    ("all", from_before),
                    ("all", gq),
                    ("all", gk),
                    ("any", gv),
                ],
                [("all", packed, f32), ("all", packed, f32), ("head", per_head, f32)],
                heads=heads,
                aliases={13: 2} if heads[0] else None,
            )
        )

    empty = jnp.zeros((8, 128), f32)
    chain.step()
    down.step()
    grads = back((0, HEADS // 2), empty, empty, empty)
    lay2, *lay3 = fence(lay2, *lay3)
    far_lay = over_x(low_sum([lay2, jnp.concatenate(lay3)]))
    chain.step()
    down.step()
    gate.step()
    up = Task(line, wide_share(*fence(*up_parts)))
    grad_mixed_low, *copies = fence(grad_mixed_low, *copies)
    out = []
    for place, order in enumerate((("y", "seq"), ("seq", "y"))):
        pieces = fence(
            *core_grad(
                bits,
                fence(mixed_low),
                mixed_low1,
                grad_mixed_low,
                copies,
                place,
                2,
                nseq,
                True,
            )
        )
        out.append(Task(line, share(pieces, True, order)))
    gq, gk_part, gv_part = back((HEADS // 2, HEADS), *grads)
    states = chain.drain()
    gate.step()
    down.step()
    grad_keys, grad_values_low = head_call(
        back_state_kernel,
        [
            ("smem", jnp.ones((nseq - 1,), f32)),
            *tables,
            ("all", keys),
            ("head", values),
            ("all", at_end),
            ("all", gk_part),
            ("head", gv_part),
            *(("state", s) for s in states),
        ],
        [("all", packed, bf16), ("head", per_head, bf16)],
        scratch=[pltpu.VMEM(packed, f32)],
    )
    grad_queries = gq.astype(bf16)
    half = (width + 2 * w_query.shape[1]) // 2
    grad_all = fence(
        grad_values_low[:, :half],
        jnp.concatenate([grad_values_low[:, half:], grad_queries, grad_keys], axis=-1),
    )
    up.step()
    grad_all1 = [over_feat(g) for g in grad_all]
    inner = []
    for own, other, (along_x, order) in zip(
        grad_all, grad_all1, ((False, ("x", "seq")), (True, ("y", "seq")))
    ):
        pieces = fence(
            *core_grad(bits, low_one, low_one1, own, [fence(other)], 0, 1, nseq, along_x)
        )
        inner.append(Task(line, share(pieces, along_x, order)))
    gate.step()
    layer_out = fence(middle + total_of([lay0, jnp.concatenate(lay1), fence(far_lay)]))
    grad_low_one = fence(
        mm(fence(grad_queries), w_query, NT)
        + mm(grad_keys, w_key, NT)
        + mm(grad_values_low, w_value, NT)
    )
    up.step()
    out[0].step()
    out[1].step()
    unit_one = flat * root_one
    grad_gain_one = jnp.sum(grad_low_one * unit_one, axis=0)
    scaled = grad_low_one * gain_one
    grad_tokens = grad_middle + root_one * (
        scaled - unit_one * jnp.mean(scaled * unit_one, axis=-1, keepdims=True)
    )
    grad_tokens, grad_gain_one = fence(grad_tokens, grad_gain_one)
    both = jnp.concatenate(
        [grad_gain_one.reshape(-1, part), gains_two[0].reshape(-1, part)], axis=-1
    )
    both = lax.all_to_all(both, ("feat", "seq", "rows"), 0, 0, tiled=True)
    tasks = [*inner, up, *out, gate, down]
    while not all(t.done for t in tasks):
        for t in tasks:
            t.step()
    gains = jnp.sum(fence(both), axis=0) + line.mark
    grad_out_w = jnp.concatenate([t.result for t in out], axis=-1)
    qk = w_query.shape[1]
    lower, upper = (t.result for t in inner)

    return (
        layer_out.reshape(rows_dev, stretch, width),
        grad_tokens.reshape(rows_dev, stretch, width),
        gains[:part],
        upper[:, width - half : width - half + qk],
        upper[:, width - half + qk :],
        jnp.concatenate([lower, upper[:, : width - half]], axis=-1),
        grad_out_w,
        gains[part:],
        gate.result,
        up.result,
        down.result,
    )


def solution(mesh):
    split = P(("feat", "rows"), "seq", None)
    vector = P(("feat", "seq", "rows"))
    matrix = P(("feat", "seq", "rows"), None)
    in_specs = (split, *(P() for _ in range(10)), split)
    out_specs = (
        split,
        split,
        vector,
        matrix,
        matrix,
        matrix,
        matrix,
        vector,
        matrix,
        matrix,
        matrix,
    )
    return jax.shard_map(shards, mesh=mesh, in_specs=in_specs, out_specs=out_specs, check_vma=False)
```

```python
import functools

import jax
import jax.numpy as jnp
import ml_dtypes
import numpy as np
from jax import lax
from jax.experimental import pallas as pl
from jax.experimental.pallas import tpu as pltpu
from jax.sharding import PartitionSpec as P

HEADS = 16
FDIM = 16
VHEAD = 128
EPS = 1e-06

bf16 = jnp.bfloat16
f32 = jnp.float32

PAIRS = [(a, b) for a in range(FDIM + 1) for b in range(a, FDIM + 1)]
NPAIR = len(PAIRS)
PADF = 256
STATE_ROWS = 160
VMEM_MIB = 30
bf16 = jnp.bfloat16
f32 = jnp.float32

PAIRS = [(a, b) for a in range(FDIM + 1) for b in range(a, FDIM + 1)]
NPAIR = len(PAIRS)
PADF = 256
STATE_ROWS = 160
VMEM_MIB = 30
SCALE = 20

NN = (((1,), (0,)), ((), ()))
NT = (((1,), (1,)), ((), ()))
TN = (((0,), (0,)), ((), ()))


def mm(a, b, dims=NN):
    return lax.dot_general(a, b, dims, preferred_element_type=f32)


def feature_tables():
    level = np.zeros((8, PADF), np.float32)
    for f, (a, b) in enumerate(PAIRS):
        level[0, f] = float(a == FDIM)
        level[1, f] = float(b == FDIM)
        if a == FDIM:
            level[2, f] = 1.0
        elif b == FDIM:
            level[2, f] = FDIM**-0.5
        elif a == b:
            level[2, f] = 1.0 / (2 * FDIM)
        else:
            level[2, f] = 1.0 / FDIM
    pick = np.zeros((2, HEADS, HEADS * FDIM, PADF), np.float32)
    for head in range(HEADS):
        for f, pair in enumerate(PAIRS):
            for k, entry in enumerate(pair):
                if entry < FDIM:
                    pick[k, head, head * FDIM + entry, f] = 1.0
    pick = pick.astype(ml_dtypes.bfloat16)
    return jnp.asarray(pick[0]), jnp.asarray(pick[1]), jnp.asarray(level)


FREE = pl.CostEstimate(flops=0, bytes_accessed=0, transcendentals=0)


def params(mib):
    return pltpu.CompilerParams(vmem_limit_bytes=mib << 20)


def factors(packed, pick_a, pick_b, level):
    return mm(packed, pick_a[0]) + level[0:1, :], mm(packed, pick_b[0]) + level[1:2, :]


def wide(value, times):
    return jnp.concatenate([value] * times, axis=1)


def parts(value):
    high = value.astype(bf16)
    return high, (value - high.astype(f32)).astype(bf16)


def own_lanes(head, packed):
    lane = lax.broadcasted_iota(jnp.int32, packed.shape, 1)
    return jnp.where(lane // FDIM == head, packed, jnp.zeros_like(packed))


def pack_state(state, sums):
    block = state[:STATE_ROWS]
    high = sums.astype(bf16).astype(f32)
    low = sums - high
    row = lax.broadcasted_iota(jnp.int32, block.shape, 0)
    for k, part in enumerate((high[:, :128], high[:, 128:], low[:, :128], low[:, 128:])):
        block = jnp.where(row == NPAIR + k, part, block)
    return block.astype(bf16)


def unpack_state(block):
    row = lax.broadcasted_iota(jnp.int32, block.shape, 0)

    def line(k):
        return jnp.sum(jnp.where(row == NPAIR + k, block, 0.0), axis=0, keepdims=True)

    sums = jnp.concatenate([line(0) + line(2), line(1) + line(3)], axis=1)
    state = jnp.where(row < NPAIR, block, 0.0).astype(bf16)
    pad = jnp.zeros((PADF - STATE_ROWS, VHEAD), bf16)
    return jnp.concatenate([state, pad], axis=0), sums


def sum_against(feats, sums):
    return sum(mm(feats, p, NT) for p in parts(jnp.broadcast_to(sums, (128, PADF))))


def column(ref, head):
    row = lax.broadcasted_iota(jnp.int32, (128, 128), 0)
    pick = jnp.where(row == head, 1.0, 0.0).astype(bf16)
    return sum(mm(p, pick) for p in parts(ref[...]))


def row_sum(value):
    ones = jnp.ones((128, 128), bf16)
    return sum(mm(p, ones) for p in parts(value))


def set_column(ref, head, value):
    lane = lax.broadcasted_iota(jnp.int32, ref.shape, 1)

    @pl.when(head == 0)
    def _():
        ref[...] = jnp.zeros_like(ref)

    ref[...] = jnp.where(lane == head, value, ref[...])


def key_state_kernel(head, pick_a, pick_b, level, k_ref, v_ref, end_ref, out_ref):
    one, two = factors(k_ref[...], pick_a, pick_b, level)
    feats = (one * two * wide(end_ref[...], 2)).astype(bf16)
    state = mm(feats, v_ref[...], TN)
    sums = jnp.sum(feats.astype(f32), axis=0, keepdims=True)
    out_ref[0] = pack_state(state, sums)


def intra_kernel(head, pick_a, pick_b, level, q_ref, k_ref, v_ref, mask_ref, num_ref, den_ref, feat_ref):
    queries = q_ref[...]
    scores = mm(own_lanes(head, queries), k_ref[...], NT)
    lin = scores * 0.25 + 1.0
    weights = ((lin * lin * 0.5 + 0.5) * mask_ref[...]).astype(bf16)
    values = v_ref[...]
    both = mm(weights, jnp.concatenate([values, jnp.ones_like(values)], axis=1))
    num_ref[...] = both[:, :VHEAD]
    set_column(den_ref, head, both[:, VHEAD:])
    one, two = factors(queries, pick_a, pick_b, level)
    feat_ref[0] = (one * two * level[2:3, :]).astype(bf16)


def kept_state(kept_ref, state_refs):
    block = jnp.zeros(state_refs[0].shape[1:], f32)
    for k, ref in enumerate(state_refs):
        block = block + kept_ref[k] * ref[0].astype(f32)
    return block


def combine_kernel(head, kept_ref, feat_ref, num_ref, den_ref, from_ref, *refs):
    *state_refs, mixed_ref, total_ref, block_ref = refs
    feats = feat_ref[0]
    block = kept_state(kept_ref, state_refs)
    block_ref[0] = block
    state, sums = unpack_state(block)
    reach = from_ref[...]
    den = column(den_ref, head) + reach * sum_against(feats, sums)
    mixed_ref[...] = ((num_ref[...] + reach * mm(feats, state)) * (1.0 / den)).astype(bf16)
    set_column(total_ref, head, den)


def query_state_kernel(
    head, feat_ref, grad_ref, mixed_ref, den_ref, from_ref, out_ref, gnum_ref, gden_ref
):
    feats = feat_ref[0]
    gnum = (grad_ref[...] * (1.0 / column(den_ref, head))).astype(bf16)
    far = gnum.astype(f32)
    gden = -row_sum(far * mixed_ref[...].astype(f32))
    reach = from_ref[...]
    state = mm(feats, (far * reach).astype(bf16), TN)
    sums = jnp.sum(feats.astype(f32) * wide(gden * reach, 2), axis=0, keepdims=True)
    out_ref[0] = pack_state(state, sums)
    gnum_ref[...] = gnum
    set_column(gden_ref, head, gden)


def back_kernel(
    first,
    head,
    pick_a,
    pick_b,
    level,
    q_ref,
    k_ref,
    v_ref,
    mask_ref,
    gnum_ref,
    gden_ref,
    state_ref,
    from_ref,
    gq_in,
    gk_in,
    gv_in,
    gq_ref,
    gk_ref,
    gv_ref,
):
    queries, keys, values = q_ref[...], k_ref[...], v_ref[...]
    gnum = gnum_ref[...]
    gden = column(gden_ref, head)
    q_own, k_own = own_lanes(head, queries), own_lanes(head, keys)
    scores = mm(q_own, keys, NT)
    lin = scores * 0.25 + 1.0
    mask = mask_ref[...]
    weights = ((lin * lin * 0.5 + 0.5) * mask).astype(bf16)
    spread = wide(gden, keys.shape[0] // 128)
    slopes = ((mm(gnum, values, NT) + spread) * (mask * lin * 0.25)).astype(bf16)
    gv_ref[...] = mm(weights, gnum, TN)
    grad_q = mm(slopes, k_own)
    grad_k = mm(slopes, q_own, TN)

    one, two = factors(queries, pick_a, pick_b, level)
    state, sums = unpack_state(state_ref[0])
    reach = from_ref[...]
    gfeat = (mm(gnum, state, NT) + wide(gden, 2) * sums) * wide(reach, 2) * level[2:3, :]
    grad_q += mm((gfeat * two).astype(bf16), pick_a[0], NT)
    grad_q += mm((gfeat * one).astype(bf16), pick_b[0], NT)

    @pl.when(head == first)
    def _():
        if first == 0:
            gq_ref[...] = jnp.zeros_like(gq_ref)
            gk_ref[...] = jnp.zeros_like(gk_ref)
        else:
            gq_ref[...] = gq_in[...]
            gk_ref[...] = gk_in[...]

    gq_ref[...] += grad_q
    gk_ref[...] += grad_k


def back_state_kernel(
    head, kept_ref, pick_a, pick_b, level, k_ref, v_ref, end_ref, gk_in, gv_in, *refs
):
    *state_refs, gk_ref, gv_ref, gk_sum = refs
    values = v_ref[...]
    one, two = factors(k_ref[...], pick_a, pick_b, level)
    state, sums = unpack_state(kept_state(kept_ref, state_refs))
    reach = wide(end_ref[...], 2)
    feats = (one * two * reach).astype(bf16)
    gv_ref[...] = (gv_in[...] + mm(feats, state)).astype(bf16)
    gfeat = (mm(values, state, NT) + sums) * reach
    grad_k = mm((gfeat * two).astype(bf16), pick_a[0], NT)
    grad_k += mm((gfeat * one).astype(bf16), pick_b[0], NT)

    @pl.when(head == 0)
    def _():
        gk_sum[...] = gk_in[...]

    gk_sum[...] += grad_k

    @pl.when(head == HEADS - 1)
    def _():
        gk_ref[...] = gk_sum[...].astype(bf16)


def head_call(kernel, ins, outs, heads=(0, HEADS), scratch=(), aliases=None):
    first, last = heads

    def spec(kind, shape):
        if kind == "all":
            return pl.BlockSpec(shape, lambda h: (0,) * len(shape))
        if kind == "head":
            return pl.BlockSpec((shape[0], VHEAD), lambda h: (0, h + first))
        if kind == "state":
            return pl.BlockSpec((1, *shape[1:]), lambda h: (h + first, 0, 0))
        if kind == "smem":
            return pl.BlockSpec(memory_space=pltpu.SMEM)
        return pl.BlockSpec(memory_space=pl.ANY)

    def body(*refs):
        kernel(pl.program_id(0) + first, *refs)

    return pl.pallas_call(
        body,
        grid=(last - first,),
        in_specs=[spec(kind, a.shape) for kind, a in ins],
        out_specs=[spec(kind, shape) for kind, shape, _ in outs],
        out_shape=[sds(shape, dtype) for _, shape, dtype in outs],
        scratch_shapes=list(scratch),
        input_output_aliases=aliases or {},
        compiler_params=params(20),
        cost_estimate=FREE,
    )(*(a for _, a in ins))


def sds(shape, dtype):
    return jax.ShapeDtypeStruct(shape, dtype)


def hidden_grad_kernel(half, which_ref, g0, g1, wd, out):
    branch = jnp.where(pl.program_id(0) < half, g0[...], g1[...])
    out[...] = mm(branch, wd[...], NT).astype(bf16)


def act_kernel(half, which_ref, x0, x1, grad_ref, wg, wu, hid, gg, gu):
    tokens = jnp.where(pl.program_id(0) < half, x0[...], x1[...])
    gate = mm(tokens, wg[...])
    up = mm(tokens, wu[...])
    grad = grad_ref[...].astype(f32)
    sig = 1.0 / (1.0 + jnp.exp(-gate))
    silu = gate * sig
    hid[...] = (silu * up).astype(bf16)
    gg[...] = (grad * up * (sig * (1.0 + gate * (1.0 - sig)))).astype(bf16)
    gu[...] = (grad * silu).astype(bf16)


def put(half, value, low, pieces):
    step = pl.program_id(0)

    @pl.when(step < half)
    def _():
        low[...] = value

    for k, piece in enumerate(pieces):
        here = step == half + k if len(pieces) > 1 else step >= half

        @pl.when(here)
        def _(piece=piece):
            piece[...] = value


def low_grad_kernel(half, which_ref, gg, gu, wg, wu, low, *pieces):
    value = (mm(gg[...], wg[...], NT) + mm(gu[...], wu[...], NT)).astype(bf16)
    put(half, value, low, pieces)


def layer_kernel(half, which_ref, hid, wd, low, *pieces):
    put(half, mm(hid[...], wd[...]).astype(bf16), low, pieces)


def token_call(kernel, which, count, ins, outs, width, slice_ff):
    tile = min(256, count)
    half = count // tile
    once = pl.Buffered(1)
    low = pl.BlockSpec((tile, width), lambda i, w: (jnp.minimum(i, half - 1), 0))
    high = pl.BlockSpec((tile, width), lambda i, w: (jnp.maximum(i - half, 0), 0))
    row = pl.BlockSpec((tile, slice_ff), lambda i, w: (i, 0))
    specs, operands = [], []
    for kind, *arrays in ins:
        operands += arrays
        specs += {
            "pair": [low, high],
            "row": [row],
            "wide": [pl.BlockSpec((width, slice_ff), lambda i, w: (0, w[0]), pipeline_mode=once)],
            "tall": [pl.BlockSpec((slice_ff, width), lambda i, w: (w[0], 0), pipeline_mode=once)],
        }[kind]
    out_specs, out_shapes = [], []
    for kind in outs:
        if kind == "row":
            out_specs.append(row)
            out_shapes.append(sds((2 * count, slice_ff), bf16))
        elif kind == "two":
            out_specs += [low, high]
            out_shapes += [sds((count, width), bf16)] * 2
        else:
            piece = pl.BlockSpec((tile, width), lambda i, w: (0, 0))
            out_specs += [low] + [piece] * half
            out_shapes += [sds((count, width), bf16)] + [sds((tile, width), bf16)] * half
    return pl.pallas_call(
        functools.partial(kernel, half),
        grid_spec=pltpu.PrefetchScalarGridSpec(
            num_scalar_prefetch=1,
            grid=(2 * half,),
            in_specs=specs,
            out_specs=out_specs,
        ),
        out_shape=out_shapes,
        compiler_params=params(VMEM_MIB),
        cost_estimate=FREE,
    )(which, *operands)


def split_rows(total, high, send, keep):
    groups = send.shape[0]
    rows = total.shape[0] // groups
    for g in range(groups):
        a = total[g * rows : g * rows + rows // 2]
        b = total[g * rows + rows // 2 : (g + 1) * rows]
        send[g] = jnp.where(high, a, b).astype(bf16)
        keep[g] = jnp.where(high, b, a).astype(bf16)


def wide_grad_kernel(ybit_ref, l0, l1, l2, l3, near, far, send, keep):
    count = l0.shape[0]
    total = mm(l0[...], near[:count, :], TN)
    total += mm(l1[...], near[count:, :], TN)
    total += mm(l2[...], far[:count, :], TN)
    total += mm(l3[...], far[count:, :], TN)
    split_rows(total, ybit_ref[0] == 1, send, keep)


def wide_grad(ybit, lows, near, far, group_rows):
    count, width = lows[0].shape
    cols = near.shape[1]
    tile = min(256, width)
    groups = tile // group_rows
    lane = pl.BlockSpec((count, tile), lambda i, w: (0, i))
    held = pl.BlockSpec((2 * count, cols), lambda i, w: (0, 0), pipeline_mode=pl.Buffered(1))
    out = pl.BlockSpec((groups, group_rows // 2, cols), lambda i, w: (i, 0, 0))
    shape = sds((width // group_rows, group_rows // 2, cols), bf16)
    return pl.pallas_call(
        wide_grad_kernel,
        grid_spec=pltpu.PrefetchScalarGridSpec(
            num_scalar_prefetch=1,
            grid=(width // tile,),
            in_specs=[lane, lane, lane, lane, held, held],
            out_specs=[out, out],
        ),
        out_shape=[shape, shape],
        compiler_params=params(VMEM_MIB),
        cost_estimate=FREE,
    )(ybit, *lows, near, far)


def down_grad_kernel(ybit_ref, near, far, g0, g1, g2, g3, send, keep):
    count = g0.shape[0]
    total = mm(near[:count, :], g0[...], TN)
    total += mm(near[count:, :], g1[...], TN)
    total += mm(far[:count, :], g2[...], TN)
    total += mm(far[count:, :], g3[...], TN)
    split_rows(total, ybit_ref[0] == 1, send, keep)


def down_grad(ybit, near, far, grads, group_rows):
    count, width = grads[0].shape
    rows = near.shape[1]
    tile = min(256, width)
    lane = pl.BlockSpec((count, tile), lambda i, w: (0, i))
    held = pl.BlockSpec((2 * count, rows), lambda i, w: (0, 0), pipeline_mode=pl.Buffered(1))
    out = pl.BlockSpec((rows // group_rows, group_rows // 2, tile), lambda i, w: (0, 0, i))
    shape = sds((rows // group_rows, group_rows // 2, width), bf16)
    return pl.pallas_call(
        down_grad_kernel,
        grid_spec=pltpu.PrefetchScalarGridSpec(
            num_scalar_prefetch=1,
            grid=(width // tile,),
            in_specs=[held, held, lane, lane, lane, lane],
            out_specs=[out, out],
        ),
        out_shape=[shape, shape],
        compiler_params=params(VMEM_MIB),
        cost_estimate=FREE,
    )(ybit, near, far, *grads)


def norm_back_kernel(low, near, far, middle, seed, gain, w, grad_ref, low_ref, mixed_ref, gain_ref, *copies):
    grad = low[...].astype(f32) + near[...].astype(f32) + far[...].astype(f32)
    value = middle[...]
    root = lax.rsqrt(jnp.mean(value * value, axis=-1, keepdims=True) + EPS)
    unit = value * root

    @pl.when(pl.program_id(0) == 0)
    def _():
        gain_ref[...] = jnp.zeros_like(gain_ref)

    gain_ref[...] += jnp.broadcast_to(jnp.sum(grad * unit, axis=0, keepdims=True), gain_ref.shape)
    scaled = grad * gain[...]
    total = seed[...] + root * (scaled - unit * jnp.mean(scaled * unit, axis=-1, keepdims=True))
    grad_ref[...] = total
    narrow = total.astype(bf16)
    low_ref[...] = narrow
    for k, copy in enumerate(copies):

        @pl.when(pl.program_id(0) == k)
        def _(copy=copy):
            copy[...] = narrow

    mixed_ref[...] = mm(narrow, w[...], NT).astype(bf16)


def norm_back(low, near, far, middle, seed, gain, w):
    count, width = middle.shape
    tile = min(256, count)
    halves = count // tile
    row = pl.BlockSpec((tile, width), lambda i: (i, 0))

    def held(shape):
        return pl.BlockSpec(shape, lambda i: (0, 0), pipeline_mode=pl.Buffered(1))

    return pl.pallas_call(
        norm_back_kernel,
        grid=(count // tile,),
        in_specs=[row] * 5 + [held((1, width)), held(w.shape)],
        out_specs=[row] * 3
        + [pl.BlockSpec((8, width), lambda i: (0, 0))]
        + [
            pl.BlockSpec((tile, width), lambda i: (0, 0)) for _ in range(halves)
        ],
        out_shape=[
            sds((count, width), f32),
            sds((count, width), bf16),
            sds((count, width), bf16),
            sds((8, width), f32),
            *[sds((tile, width), bf16)] * halves,
        ],
        compiler_params=params(50),
        cost_estimate=FREE,
    )(low, near, far, middle, seed, gain.reshape(1, width), w)


def core_grad_kernel(along_x, bits_ref, r0, r1, c0, *refs):
    *others, send, keep = refs
    total = mm(r0[...], c0[...], TN)
    first = 0
    for c1 in others:
        count = c1.shape[0]
        total += mm(r1[first : first + count, :], c1[...], TN)
        first += count
    groups, _, rows, _ = send.shape
    high = bits_ref[1 if along_x else 2] == 1
    for g in range(groups):

        def block(y, x):
            first = (4 * g + 2 * y + x) * rows
            return total[first : first + rows]

        for k in range(2):
            a, b = (block(k, 0), block(k, 1)) if along_x else (block(0, k), block(1, k))
            send[g, k] = jnp.where(high, a, b).astype(bf16)
            keep[g, k] = jnp.where(high, b, a).astype(bf16)


def core_grad(bits, r0, r1, c0, others, place, parts, nseq, along_x):
    count, width = r0.shape
    cols = c0.shape[1] // parts
    tile = min(256, width // 2)
    steps = width // 2 // tile
    rows = width // (8 * nseq)
    groups = tile // (4 * rows)
    lane = pl.BlockSpec((count, tile), lambda i, w: (0, w[0] * steps + i))

    def held(a):
        return pl.BlockSpec(
            (a.shape[0], cols), lambda i, w: (0, place), pipeline_mode=pl.Buffered(1)
        )

    out = pl.BlockSpec((groups, 2, rows, cols), lambda i, w: (i, 0, 0, 0))
    return pl.pallas_call(
        functools.partial(core_grad_kernel, along_x),
        grid_spec=pltpu.PrefetchScalarGridSpec(
            num_scalar_prefetch=1,
            grid=(steps,),
            in_specs=[lane, lane, held(c0), *(held(c) for c in others)],
            out_specs=[out, out],
        ),
        out_shape=[sds((nseq, 2, rows, cols), bf16)] * 2,
        compiler_params=params(VMEM_MIB),
        cost_estimate=FREE,
    )(bits, r0, r1, c0, *others)


def total_of(terms):
    total = terms[0].astype(f32)
    for term in terms[1:]:
        total = total + term.astype(f32)
    return total


def take(terms, dim, place):
    return [lax.dynamic_index_in_dim(t, place, dim, keepdims=False) for t in terms]


class Line:
    def __init__(self, mark):
        self.mark = mark

    def fence(self, *values):
        *values, self.mark = lax.optimization_barrier((*values, self.mark))
        return values[0] if len(values) == 1 else tuple(values)


class Task:
    def __init__(self, line, chain):
        self.line, self.chain, self.done = line, chain, False
        self.result = None
        self.waiting = next(chain)

    def step(self, count=1):
        for _ in range(count):
            if self.done:
                return
            try:
                self.waiting = self.chain.send(self.line.fence(self.waiting))
            except StopIteration as end:
                self.done, self.result = True, end.value

    def drain(self):
        while not self.done:
            self.step()
        return self.result


def shards(
    tokens,
    lengths,
    gain_one,
    w_query,
    w_key,
    w_value,
    w_out,
    gain_two,
    w_gate,
    w_up,
    w_down,
    cotangent,
):
    rows_dev, stretch, width = tokens.shape
    nfeat, nseq, nrows = (lax.axis_size(a) for a in ("feat", "seq", "rows"))
    assert rows_dev == 1 and nfeat == 2 and nrows == 4 and nseq % 2 == 0
    ff = w_gate.shape[1]
    fi, si, ri = (lax.axis_index(a) for a in ("feat", "seq", "rows"))
    xb, yb = ri % 2, ri // 2
    slice_ff = ff // 4
    which = jnp.reshape(2 * fi + xb, (1,)).astype(jnp.int32)
    ybit = jnp.reshape(yb, (1,)).astype(jnp.int32)
    bits = jnp.stack([fi, xb, yb]).astype(jnp.int32)

    line = Line((lengths[0, :1] < 0).astype(f32))
    fence = line.fence

    def over_feat(a):
        return lax.ppermute(a, "feat", [(0, 1), (1, 0)])

    def over_x(a):
        return lax.ppermute(a, "rows", [(r, r ^ 1) for r in range(nrows)])

    def over_y(a):
        return lax.ppermute(a, "rows", [(r, r ^ 2) for r in range(nrows)])

    def over_seq(a, shift=1):
        return lax.ppermute(a, "seq", [(s, (s + shift) % nseq) for s in range(nseq)])

    depth = nseq.bit_length() - 1
    assert nseq == 1 << depth

    def over_bit(k, a):
        return lax.ppermute(a, "seq", [(s, s ^ (1 << k)) for s in range(nseq)])

    def hops(state):
        states = []
        for _ in range(nseq - 1):
            state = yield over_seq(state)
            states.append(state)
        return states

    def hops_back(own):
        states, state = [], own
        for last in range(nseq - 1, 0, -1):
            state = yield lax.ppermute(state, "seq", [(last, last - 1)])
            states.append(state)
            state = low_sum([own, passes * state.astype(f32)])
        return states

    def low_sum(terms):
        return total_of(terms).astype(bf16)

    def pair_step(terms, dim, bit, swap):
        arrived = yield swap(low_sum(take(terms, dim, 1 - bit)))
        return [*take(terms, dim, bit), arrived]

    def ring_step(pick):
        held = []
        for k in range(nseq - 1):
            block = lax.rem(si - 1 - k + 2 * nseq, nseq)
            arrived = yield over_seq(low_sum(pick(block) + held))
            held = [arrived]
        return pick(si) + held

    flat = tokens.reshape(stretch, width)
    seed = cotangent.reshape(stretch, width)
    branch0 = fence(seed.astype(bf16))
    branch1, branch2 = over_feat(branch0), over_x(branch0)

    ndocs = lengths.shape[1]
    doc_lengths = lax.dynamic_index_in_dim(lengths, fi * nrows + ri, 0, keepdims=False)
    starts = jnp.cumsum(doc_lengths) - doc_lengths
    offset = si * stretch

    def doc_of(places):
        return jnp.sum((starts[None, :] <= places[:, None]).astype(jnp.int32), axis=1)

    places = offset + jnp.arange(stretch, dtype=jnp.int32)
    docs = doc_of(places)
    away = jnp.arange(1, nseq, dtype=jnp.int32)
    before = doc_of(jnp.reshape(offset - 1, (1,)))
    final = doc_of(jnp.reshape(offset + stretch - 1, (1,)))
    causal = jnp.arange(stretch)[None, :] <= jnp.arange(stretch)[:, None]
    mask = ((docs[:, None] == docs[None, :]) & causal).astype(f32)
    from_before = jnp.broadcast_to((docs == before).astype(f32)[:, None], (stretch, 128))
    at_end = jnp.broadcast_to((docs == final).astype(f32)[:, None], (stretch, 128))
    earlier = (
        (doc_of(offset - 1 - (away - 1) * stretch) == before) & (away <= si)
    ).astype(f32)
    passes = (final == before).astype(f32)

    pick_a, pick_b, level = feature_tables()
    tables = [("state", pick_a), ("state", pick_b), ("all", level)]
    state_shape = (HEADS, STATE_ROWS, VHEAD)
    columns = ("all", (stretch, 128), f32)
    packed = (stretch, HEADS * FDIM)
    per_head = (stretch, width)

    root_one = lax.rsqrt(jnp.mean(flat * flat, axis=-1, keepdims=True) + EPS)
    low_one = (flat * root_one * gain_one).astype(bf16)
    low_one1 = over_feat(low_one)
    keys = mm(low_one, w_key).astype(bf16)
    values = mm(low_one, w_value).astype(bf16)
    (key_state,) = head_call(
        key_state_kernel,
        [*tables, ("all", keys), ("head", values), ("all", at_end)],
        [("state", state_shape, bf16)],
    )
    chain = Task(line, hops(fence(key_state)))
    queries = mm(fence(low_one), w_query).astype(bf16)
    numer, denom_here, feats = fence(
        *head_call(
            intra_kernel,
            [
                *tables,
                ("all", queries),
                ("all", keys),
                ("head", values),
                ("all", mask),
            ],
            [("head", per_head, f32), columns, ("state", (HEADS, stretch, PADF), bf16)],
        )
    )
    chain.step()

    def hidden_grad(g0, g1):
        return token_call(
            hidden_grad_kernel,
            which,
            stretch,
            [("pair", g0, g1), ("tall", w_down)],
            ["row"],
            width,
            slice_ff,
        )[0]

    def act(x0, x1, grad):
        return token_call(
            act_kernel,
            which,
            stretch,
            [("pair", x0, x1), ("row", grad), ("wide", w_gate), ("wide", w_up)],
            ["row"] * 3,
            width,
            slice_ff,
        )

    def low_grad(gg, gu, kind):
        return token_call(
            low_grad_kernel,
            which,
            stretch,
            [("row", gg), ("row", gu), ("wide", w_gate), ("wide", w_up)],
            [kind],
            width,
            slice_ff,
        )

    def layer(hid, kind):
        return token_call(
            layer_kernel,
            which,
            stretch,
            [("row", hid), ("tall", w_down)],
            [kind],
            width,
            slice_ff,
        )

    branch1, low_one1 = fence(branch1, low_one1)
    gh_near = fence(hidden_grad(branch0, branch1))
    chain.step()
    branch2 = fence(branch2)
    branch3 = over_feat(branch2)
    branch3 = fence(branch3)
    gh_far = fence(hidden_grad(branch2, branch3))
    states = chain.drain()

    mixed_low, denom, state_in = head_call(
        combine_kernel,
        [
            ("smem", earlier),
            ("state", feats),
            ("head", numer),
            ("all", denom_here),
            ("all", from_before),
            *(("state", s) for s in states),
        ],
        [("head", per_head, bf16), columns, ("state", state_shape, f32)],
    )
    mixed_low1 = over_feat(mixed_low)
    middle = flat + mm(mixed_low, w_out)
    root_two = lax.rsqrt(jnp.mean(middle * middle, axis=-1, keepdims=True) + EPS)
    low0 = fence((middle * root_two * gain_two).astype(bf16))
    low1, low2 = over_feat(low0), over_x(low0)

    mixed_low1, low1 = fence(mixed_low1, low1)
    hid_n, gg_n, gu_n = fence(*act(low0, low1, gh_near))
    glow0, glow1 = fence(*low_grad(gg_n, gu_n, "two"))
    glow1 = over_feat(glow1)
    low2 = fence(low2)
    low3 = over_feat(low2)
    low3, glow1 = fence(low3, glow1)
    hid_f, gg_f, gu_f = fence(*act(low2, low3, gh_far))

    lows = (low0, low1, low2, low3)
    branches = (branch0, branch1, branch2, branch3)
    group_rows = width // (2 * nseq)

    def wide_share(sent, kept):
        terms = [kept, (yield over_y(sent))]
        split = [t.reshape(2, nseq, 2, group_rows // 4, slice_ff) for t in terms]
        mine = yield from ring_step(lambda b: take(split, 1, b))
        mine = total_of(mine).astype(bf16)
        own = lax.dynamic_index_in_dim(mine, xb, 1, keepdims=False)
        other = yield over_x(lax.dynamic_index_in_dim(mine, 1 - xb, 1, keepdims=False))
        cols = jnp.where(
            xb == 0,
            jnp.concatenate([own, other], axis=-1),
            jnp.concatenate([other, own], axis=-1),
        )
        own = lax.dynamic_index_in_dim(cols, fi, 0, keepdims=False)
        other = yield over_feat(lax.dynamic_index_in_dim(cols, 1 - fi, 0, keepdims=False))
        return fence(
            jnp.where(
                fi == 0,
                jnp.concatenate([own, other], axis=-1),
                jnp.concatenate([other, own], axis=-1),
            ).astype(f32)
        )

    def down_share(sent, kept):
        rows = slice_ff // (2 * nseq)
        terms = [kept, (yield over_y(sent))]
        split = [t.reshape(nseq // 2, 2, rows, width) for t in terms]

        def pick(b):
            zero = jnp.int32(0)
            place = (b % (nseq // 2), b // (nseq // 2), zero, zero)
            return [
                lax.dynamic_slice(t, place, (1, 1, rows, width)).reshape(rows, width)
                for t in split
            ]

        mine = yield from ring_step(pick)
        mine = low_sum(mine)
        swaps = []
        for s in range(nseq):
            for r in range(nrows):
                x = s // (nseq // 2)
                if x != r % 2:
                    to = (r % 2) * (nseq // 2) + s % (nseq // 2)
                    swaps.append((s * nrows + r, to * nrows + (r ^ 1)))
        moved = yield lax.ppermute(mine, ("seq", "rows"), swaps)
        stays = (si // (nseq // 2)) == xb
        return fence(jnp.where(stays, mine, moved).astype(f32))

    down_parts = fence(
        *down_grad(ybit, fence(hid_n), hid_f, branches, slice_ff // (nseq // 2))
    )
    down = Task(line, down_share(*down_parts))
    glow2, *glow3 = fence(*low_grad(fence(gg_f), gu_f, "pair"))
    glow3 = [over_feat(g) for g in glow3]
    gate_parts = fence(*wide_grad(ybit, lows, fence(gg_n), gg_f, group_rows))
    glow2, *glow3 = fence(glow2, *glow3)
    far_glow = over_x(low_sum([glow2, jnp.concatenate(glow3)]))
    up_parts = fence(*wide_grad(ybit, lows, fence(gu_n), gu_f, group_rows))
    down.step()
    gate = Task(line, wide_share(*fence(*gate_parts)))
    lay0, *lay1 = fence(*layer(fence(hid_n), "pair"))
    lay1 = [over_feat(a) for a in lay1]

    grad_middle, grad_mixed_low, grad_mixed, gains_two, *copies = fence(
        *norm_back(glow0, glow1, fence(far_glow), middle, seed, gain_two, w_out)
    )
    copies = [over_feat(a) for a in copies]
    lay1 = list(fence(lay0, *lay1)[1:])

    query_state, gnum, gden = fence(
        *head_call(
            query_state_kernel,
            [
                ("state", feats),
                ("head", fence(grad_mixed)),
                ("head", mixed_low),
                ("all", denom),
                ("all", from_before),
            ],
            [("state", state_shape, bf16), ("head", per_head, bf16), columns],
        )
    )
    chain = Task(line, hops_back(query_state))
    down.step()
    lay2, *lay3 = fence(*layer(fence(hid_f), "pair"))
    lay3 = [over_feat(a) for a in lay3]

    part = width // (8 * nseq)

    def share(parts, along_x, order):
        sent, keep = parts
        terms = [keep, (yield (over_x if along_x else over_y)(sent))]
        dims = {"seq": 0, "y" if along_x else "x": 1}
        for name in order:
            dim = dims.pop(name)
            dims = {k: v - (v > dim) for k, v in dims.items()}
            if name == "seq":
                terms = [t.reshape(*t.shape[:dim], *[2] * depth, *t.shape[dim + 1 :]) for t in terms]
                for k in range(depth):
                    terms = yield from pair_step(
                        terms, dim + depth - 1 - k, (si >> k) & 1, functools.partial(over_bit, k)
                    )
            else:
                bit, swap = {"x": (xb, over_x), "y": (yb, over_y)}[name]
                terms = yield from pair_step(terms, dim, bit, swap)
        return fence(total_of(terms))

    def back(heads, gq, gk, gv):
        return fence(
            *head_call(
                functools.partial(back_kernel, heads[0]),
                [
                    *tables,
                    ("all", queries),
                    ("all", keys),
                    ("head", values),
                    ("all", mask),
                    ("head", fence(gnum)),
                    ("all", gden),
                    ("state", state_in),
                    ("all", from_before),
                    ("all", gq),
                    ("all", gk),
                    ("any", gv),
                ],
                [("all", packed, f32), ("all", packed, f32), ("head", per_head, f32)],
                heads=heads,
                aliases={13: 2} if heads[0] else None,
            )
        )

    empty = jnp.zeros((8, 128), f32)
    chain.step()
    down.step()
    grads = back((0, HEADS // 2), empty, empty, empty)
    lay2, *lay3 = fence(lay2, *lay3)
    far_lay = over_x(low_sum([lay2, jnp.concatenate(lay3)]))
    chain.step()
    down.step()
    gate.step()
    up = Task(line, wide_share(*fence(*up_parts)))
    grad_mixed_low, *copies = fence(grad_mixed_low, *copies)
    out = []
    for place, order in enumerate((("y", "seq"), ("seq", "y"))):
        pieces = fence(
            *core_grad(
                bits,
                fence(mixed_low),
                mixed_low1,
                grad_mixed_low,
                copies,
                place,
                2,
                nseq,
                True,
            )
        )
        out.append(Task(line, share(pieces, True, order)))
    gq, gk_part, gv_part = back((HEADS // 2, HEADS), *grads)
    states = chain.drain()
    gate.step()
    down.step()
    grad_keys, grad_values_low = head_call(
        back_state_kernel,
        [
            ("smem", jnp.ones((nseq - 1,), f32)),
            *tables,
            ("all", keys),
            ("head", values),
            ("all", at_end),
            ("all", gk_part),
            ("head", gv_part),
            *(("state", s) for s in states),
        ],
        [("all", packed, bf16), ("head", per_head, bf16)],
        scratch=[pltpu.VMEM(packed, f32)],
    )
    grad_queries = gq.astype(bf16)
    half = (width + 2 * w_query.shape[1]) // 2
    grad_all = fence(
        grad_values_low[:, :half],
        jnp.concatenate([grad_values_low[:, half:], grad_queries, grad_keys], axis=-1),
    )
    up.step()
    grad_all1 = [over_feat(g) for g in grad_all]
    inner = []
    for own, other, (along_x, order) in zip(
        grad_all, grad_all1, ((False, ("x", "seq")), (True, ("y", "seq")))
    ):
        pieces = fence(
            *core_grad(bits, low_one, low_one1, own, [fence(other)], 0, 1, nseq, along_x)
        )
        inner.append(Task(line, share(pieces, along_x, order)))
    gate.step()
    layer_out = fence(middle + total_of([lay0, jnp.concatenate(lay1), fence(far_lay)]))
    up.step()
    grad_low_one = fence(
        mm(fence(grad_queries), w_query, NT)
        + mm(grad_keys, w_key, NT)
        + mm(grad_values_low, w_value, NT)
    )
    out[0].step()
    out[1].step()
    unit_one = flat * root_one
    grad_gain_one = jnp.sum(grad_low_one * unit_one, axis=0)
    scaled = grad_low_one * gain_one
    grad_tokens = grad_middle + root_one * (
        scaled - unit_one * jnp.mean(scaled * unit_one, axis=-1, keepdims=True)
    )
    grad_tokens, grad_gain_one = fence(grad_tokens, grad_gain_one)
    both = jnp.concatenate(
        [grad_gain_one.reshape(-1, part), gains_two[0].reshape(-1, part)], axis=-1
    )
    both = lax.all_to_all(both, ("feat", "seq", "rows"), 0, 0, tiled=True)
    tasks = [*inner, up, *out, gate, down]
    while not all(t.done for t in tasks):
        for t in tasks:
            t.step()
    gains = jnp.sum(fence(both), axis=0) + line.mark
    grad_out_w = jnp.concatenate([t.result for t in out], axis=-1)
    qk = w_query.shape[1]
    lower, upper = (t.result for t in inner)

    return (
        layer_out.reshape(rows_dev, stretch, width),
        grad_tokens.reshape(rows_dev, stretch, width),
        gains[:part],
        upper[:, width - half : width - half + qk],
        upper[:, width - half + qk :],
        jnp.concatenate([lower, upper[:, : width - half]], axis=-1),
        grad_out_w,
        gains[part:],
        gate.result,
        up.result,
        down.result,
    )


def solution(mesh):
    split = P(("feat", "rows"), "seq", None)
    vector = P(("feat", "seq", "rows"))
    matrix = P(("feat", "seq", "rows"), None)
    in_specs = (split, *(P() for _ in range(10)), split)
    out_specs = (
        split,
        split,
        vector,
        matrix,
        matrix,
        matrix,
        matrix,
        vector,
        matrix,
        matrix,
        matrix,
    )
    return jax.shard_map(shards, mesh=mesh, in_specs=in_specs, out_specs=out_specs, check_vma=False)
```
